256 devices in a mesh: scene: 8 (over x, core), leaf: 32 (over y, z).
Axes of the slice: x: 4, y: 4, z: 8, core: 2. Of those that a mesh axis runs over, the one named last changes fastest.
Arguments:
- leaves: bfloat16 [8, 256, 8, 8, 8, 128], P('scene', 'leaf'), may hold values from -6 to 6
- counts: int32 [8, 32], P('scene', 'leaf'), may hold values from 1 to 8, as said below
- nbr_owner: int32 [8, 256, 7], P('scene', 'leaf'), may hold values from 0 to 31, all different within a row; in each aligned block of 8 rows (0 to 7, 8 to 15, ..., all dimensions but the last counted through in order) at most 4 rows name the same one
- nbr_slot: int32 [8, 256, 7], P('scene', 'leaf'), may hold values from 0 to 7
- weight: bfloat16 [3456, 256], replicated, may hold values from -0.109375 to 0.109375
- cotangent: bfloat16 [8, 256, 4, 4, 4, 256], P('scene', 'leaf'), may hold values from -6 to 6
Outputs:
- output: bfloat16 [8, 256, 4, 4, 4, 256], P('scene', 'leaf')
- grad_leaves: bfloat16 [8, 256, 8, 8, 8, 128], P('scene', 'leaf')
- grad_weight: float32 [3456, 256], P('leaf')
The draws below stay inside these ranges and needn't reach their ends.
Inputs may be any that keep to these rules, and one draw needn't show every extreme that they name: `nbr_owner`: within the rows of one device, no owner is named by more than 4 rows, and some device names one owner in exactly 4 rows. `counts`: the live slots of a device are its first ones; in every scene some device has all 8 slots live.
All inputs are finite; a program needn't handle non-finite values.
Results may differ from the reference program's by a relative error of at most 0.0031.
Values may be sent and summed in bfloat16 or wider, within the bound.
A program may use at most 64 MiB of HBM per device.

```python
import math
import jax
import jax.numpy as jnp
import numpy as np
from jax import lax

C_IN = 128
C_OUT = 256
EDGE = 8
LEAF_DEV = 8
HALF = 4
LEAVES = 256
CAP = 4
N_SCENE = 8
N_LEAF = 32


def draw_counts(key, part):
    key = jax.random.fold_in(key, 11)
    first_key, second_key = jax.random.split(key)
    values = jax.random.randint(first_key, (N_SCENE, N_LEAF), 1, LEAF_DEV + 1)
    full_device = jax.random.randint(second_key, (N_SCENE,), 0, N_LEAF)
    places = jnp.arange(N_LEAF, dtype=jnp.int32)[None, :]
    return jnp.where(places == full_device[:, None], LEAF_DEV, values).astype(jnp.int32)


def touch_ends(drawn, own_key, smallest, largest):
    shape = drawn.shape
    index_at = [jax.random.randint(jax.random.fold_in(own_key, axis), (), 0, shape[axis]) for axis in range(len(shape))]
    drawn = drawn.at[tuple(index_at)].set(smallest)
    longest = shape.index(max(shape))
    index_at[longest] = (index_at[longest] + 1) % shape[longest]
    return drawn.at[tuple(index_at)].set(largest)


def raised(drawn, key, source, target, parts, factor):
    owner, partner = [(jnp.arange(drawn.shape[position]) // (drawn.shape[position] // parts)).reshape([-1 if axis == position else 1 for axis in range(drawn.ndim)]) for position in (source, target)]
    chosen = jax.random.permutation(key, parts)[partner]
    strong = (owner == chosen) | (owner == (partner + parts // 2) % parts)
    return jnp.where(strong, factor * drawn, drawn)


def block_scale(stream_key, shape, cuts, least, top_value):
    loudness, own = 1.0, jax.random.fold_in(stream_key, 6)
    for position, blocks in cuts:
        draws = jnp.exp(jax.random.uniform(jax.random.fold_in(own, position), (blocks,), jnp.float32, least / len(cuts), top_value / len(cuts)))
        loudness = loudness * jnp.repeat(draws, shape[position] // blocks).reshape([-1 if axis == position else 1 for axis in range(len(shape))])
    return loudness


def shared_out(own_key, own, number, rows, number_of, top, reach, skew):
    sequence = jax.random.permutation(own_key, number_of)
    packed, ordinary = load_shares(number_of, rows * top, reach, skew, True), load_shares(number_of, rows * top, reach, skew, False)
    places = jnp.arange(number_of)

    def named(lengths, rotation):
        used = int((lengths > 0).sum())
        fixed = max(1, used // 4)
        moved = fixed + (places - fixed + rotation * (used - fixed)) % max(1, number_of - fixed)
        return jnp.zeros((number_of,), jnp.int32).at[sequence[jnp.where(places < fixed, places, moved)]].set(jnp.asarray(lengths, jnp.int32))

    lengths = jnp.where(number % 4 == 0, named(packed, number // 4), named(ordinary, number - number // 4 - 1))
    mixed = jax.random.permutation(jax.random.fold_in(own, 3), number_of)
    giver, receiver = mixed[0:number_of // 2 * 2:2], mixed[1:number_of // 2 * 2:2]
    slack = jnp.minimum(lengths[giver] - 1, reach - lengths[receiver]) // 2
    slack = jnp.where((giver == sequence[0]) | (receiver == sequence[0]) | (lengths[receiver] == 0), 0, jnp.maximum(slack, 0))
    moved = jax.random.randint(jax.random.fold_in(own, 4), (number_of // 2,), 0, 1 << 20) % (slack + 1)
    lengths = lengths.at[giver].add(-moved).at[receiver].add(moved)
    members = jnp.searchsorted(jnp.cumsum(lengths), jnp.arange(rows * top), side="right").astype(jnp.int32)
    listing = members.reshape(top, rows).T
    listing = listing[jax.random.permutation(jax.random.fold_in(own, 1), rows)]
    rotation = jax.random.randint(jax.random.fold_in(own, 2), (rows, 1), 0, top)
    return jnp.take_along_axis(listing, (jnp.arange(top)[None, :] + rotation) % top, axis=1)


def load_shares(number_of, total, reach, lean, full):
    portions = [(1 << 20) // math.isqrt(grade ** lean) + 1 for grade in range(1, number_of + 1)]
    largest = reach if full else min(reach, max(-(-total // number_of), total * portions[0] // sum(portions)))
    least = 1 if total - largest >= number_of - 1 else 0
    holding, surplus = [largest] + [least] * (number_of - 1), total - largest - least * (number_of - 1)
    while surplus > 0:
        candidates = [i for i in range(1, number_of) if holding[i] < largest] or [i for i in range(1, number_of) if holding[i] < reach]
        pool, budget = sum([portions[i] for i in candidates]), surplus
        for i in candidates:
            extra = min(reach - holding[i], max(1, budget * portions[i] // pool), surplus)
            holding[i] = holding[i] + extra
            surplus = surplus - extra
    return np.array(holding)


def bell_draw(key, dims, spread, most, shards=(), held_as=jnp.bfloat16):
    level = block_scale(key, dims, shards, -0.22, 0.18) if shards else 1.0
    entries = jax.random.normal(key, dims, jnp.float32) * spread * level
    return jnp.minimum(jnp.maximum(entries, -most), most).astype(held_as)


def bell_draw_with(key, shape, deviation, most, cuts, heavy, kind=jnp.bfloat16):
    array = deviation * jax.random.normal(key, shape, jnp.float32)
    if cuts:
        array = array * block_scale(key, shape, cuts, -0.22, 0.18)
    return jnp.clip(raised(array, jax.random.fold_in(key, 3), *heavy), -most, most).astype(kind)


def setup_inputs(seed: int = 0) -> dict:
    key_of = jax.random.split(jax.random.key(seed), 7)
    leaves = bell_draw_with(key_of[0], (N_SCENE, LEAVES, EDGE, EDGE, EDGE, C_IN), 1.0, 6.0, ((0, 8), (1, 32)), (1, 5, 32, 2.75))
    counts = draw_counts(jax.random.fold_in(key_of[6], 71), 0)
    nbr_owner_keys = jax.random.split(jax.random.fold_in(key_of[2], 1), N_SCENE * LEAVES // LEAF_DEV)
    nbr_owner_turns = jax.random.permutation(jax.random.fold_in(key_of[2], 3), N_SCENE * LEAVES // LEAF_DEV)
    nbr_owner = jax.vmap(lambda own, number: shared_out(jax.random.fold_in(key_of[2], 2), own, number, LEAF_DEV, N_LEAF, 7, CAP, 2))(nbr_owner_keys, nbr_owner_turns).reshape((N_SCENE, LEAVES, 7))
    nbr_slot = touch_ends(jax.random.randint(key_of[3], (N_SCENE, LEAVES, 7), 0, LEAF_DEV), jax.random.fold_in(key_of[3], 1), 0, LEAF_DEV - 1).astype(jnp.int32)
    weight = bell_draw(key_of[4], (27 * C_IN, C_OUT), (27 * C_IN) ** -0.5, 0.109375)
    cotangent = bell_draw(key_of[5], (N_SCENE, LEAVES, HALF, HALF, HALF, C_OUT), 1.0, 6.0, ((0, 8), (1, 32)))
    return {"leaves": leaves, "counts": counts, "nbr_owner": nbr_owner, "nbr_slot": nbr_slot, "weight": weight, "cotangent": cotangent}


def direction_flags(direction):
    code_value = direction + 1
    return [code_value >> axis_id & 1 for axis_id in range(3)]

def shell_regions(flags, edge_cells):
    target = tuple((slice(0, 1) if flag else slice(1, edge_cells + 1) for flag in flags))
    source = tuple((slice(edge_cells - 1, edge_cells) if flag else slice(0, edge_cells) for flag in flags))
    return (target, source)

def tap_slices(tap_index, half_edge):
    first = tap_index // 9
    second = tap_index // 3 % 3
    third = tap_index % 3
    return (slice(None), slice(first, first + 2 * half_edge, 2), slice(second, second + 2 * half_edge, 2), slice(third, third + 2 * half_edge, 2))

def strided_forward(padded, weight, channels, half_edge):
    total = None
    for tap_index in range(27):
        patch = padded[tap_slices(tap_index, half_edge)].reshape(-1, channels)
        term = jnp.dot(patch, weight[tap_index * channels:(tap_index + 1) * channels], preferred_element_type=jnp.float32)
        total = term if total is None else total + term
    return total

def kernel_grad(padded, grad_rows, channels, half_edge):
    pieces = []
    for tap_index in range(27):
        patch = padded[tap_slices(tap_index, half_edge)].reshape(-1, channels)
        pieces.append(lax.dot_general(patch, grad_rows, (((0,), (0,)), ((), ())), preferred_element_type=jnp.float32))
    return jnp.concatenate(pieces, axis=0)

def spread_back(grad_rows, weight, leaf_total, edge_cells, channels, half_edge):
    grad_padded = jnp.zeros((leaf_total, edge_cells + 1, edge_cells + 1, edge_cells + 1, channels), jnp.float32)
    for tap_index in range(27):
        part = jnp.dot(grad_rows, weight[tap_index * channels:(tap_index + 1) * channels].T, preferred_element_type=jnp.float32)
        part = part.reshape(leaf_total, half_edge, half_edge, half_edge, channels)
        grad_padded = grad_padded.at[tap_slices(tap_index, half_edge)].add(part)
    return grad_padded

def one_scene(operands, weight):
    leaf_data, live_count, owner_ids, slot_ids, cotangent = operands
    leaf_total = leaf_data.shape[0]
    leaf_index = jnp.arange(leaf_total, dtype=jnp.int32)
    alive = leaf_index % LEAF_DEV < live_count[leaf_index // LEAF_DEV]
    alive_five = alive[:, None, None, None, None]
    masked = jnp.where(alive_five, leaf_data, jnp.zeros((), jnp.bfloat16))
    sources = (owner_ids * LEAF_DEV + slot_ids).astype(jnp.int32)
    padded = jnp.zeros((leaf_total, EDGE + 1, EDGE + 1, EDGE + 1, C_IN), jnp.bfloat16)
    padded = padded.at[:, 1:, 1:, 1:].set(masked)
    for direction in range(7):
        target, source = shell_regions(direction_flags(direction), EDGE)
        shell = masked[(slice(None),) + source][sources[:, direction]]
        padded = padded.at[(slice(None),) + target].set(shell)
    conv = strided_forward(padded, weight, C_IN, HALF).reshape(leaf_total, HALF, HALF, HALF, C_OUT)
    output = jnp.where(alive_five, conv, 0.0).astype(jnp.bfloat16)
    grad_out = jnp.where(alive_five, cotangent, jnp.zeros((), jnp.bfloat16))
    grad_rows = grad_out.reshape(-1, C_OUT)
    grad_weight = kernel_grad(padded, grad_rows, C_IN, HALF)
    grad_padded = spread_back(grad_rows, weight, leaf_total, EDGE, C_IN, HALF)
    grad_inner = grad_padded[:, 1:, 1:, 1:]
    for direction in range(7):
        target, source = shell_regions(direction_flags(direction), EDGE)
        shell_grad = grad_padded[(slice(None),) + target].astype(jnp.bfloat16)
        shell_grad = lax.optimization_barrier(shell_grad)
        grad_inner = grad_inner.at[(sources[:, direction],) + source].add(shell_grad.astype(jnp.float32))
    grad_leaves = jnp.where(alive_five, grad_inner, 0.0).astype(jnp.bfloat16)
    return (output, grad_leaves, grad_weight)

def reference(leaves, counts, nbr_owner, nbr_slot, weight, cotangent):
    outputs, grads, kernel_parts = lax.map(lambda operands: one_scene(operands, weight), (leaves, counts, nbr_owner, nbr_slot, cotangent))
    return (outputs, grads, lax.optimization_barrier(jnp.sum(kernel_parts, axis=0)))
```

```python
import functools

import jax
import jax.numpy as jnp
import numpy as np
from jax import lax
from jax.experimental import pallas as pl
from jax.experimental.pallas import tpu as pltpu
from jax.sharding import PartitionSpec as P

MESH = pl.DeviceIdType.MESH
BF = jnp.bfloat16
F32 = jnp.float32
CODES = (1, 2, 4, 3, 5, 6, 7)
SHIFTS = tuple(range(8))
HOLD = {s: [p for p in range(8) if p & s == s] for s in SHIFTS}
FIRST = {}
_at = 0
for _s in SHIFTS:
    FIRST[_s] = _at
    _at += len(HOLD[_s])


def tap_of(parity, shift):
    t = 0
    for axis in range(3):
        if not parity >> axis & 1:
            digit = 1
        elif shift >> axis & 1:
            digit = 0
        else:
            digit = 2
        t = 3 * t + digit
    return t


ORDER = [tap_of(p, s) for s in SHIFTS for p in HOLD[s]]


def base_of(d):
    return 16 * d if d < 3 else 36 + 4 * d


def cells_of(d):
    code = CODES[d]
    ranges = [[None] if code >> axis & 1 else list(range(4)) for axis in range(3)]
    return [(i, j, k) for i in ranges[0] for j in ranges[1] for k in ranges[2]]


def tables():
    perm = np.zeros((256, 256), np.float32)
    for x in range(4):
        for y in range(8):
            for z in range(8):
                p = (x & 1) + 2 * (y & 1) + 4 * (z & 1)
                perm[p * 32 + (x >> 1) * 16 + (y >> 1) * 4 + (z >> 1), x * 64 + y * 8 + z] = 1
    face = np.zeros((128, 64), np.float32)
    spread = np.zeros((128, 64), np.float32)
    place = {}
    for x in range(4):
        for y in range(4):
            for z in range(4):
                place[(x, y, z)] = 16 * x + 4 * y + z
    for d in range(7):
        for v, cell in enumerate(cells_of(d)):
            low = [0 if c is None else c for c in cell]
            face[d * 16 + v, 16 * low[0] + 4 * low[1] + low[2]] = 1
            spread[d * 16 + v, base_of(d) + v] = 1
            place[tuple(4 if c is None else c for c in cell)] = 64 + base_of(d) + v
    shift = np.zeros((7, 64, 128), np.float32)
    for s in range(1, 8):
        for x in range(4):
            for y in range(4):
                for z in range(4):
                    goal = (x + (s & 1), y + (s >> 1 & 1), z + (s >> 2 & 1))
                    shift[s - 1, 16 * x + 4 * y + z, place[goal]] = 1
    back = np.zeros((7, 512, 256), np.float32)
    for s in range(7):
        for leaf in range(4):
            back[s, leaf * 128 : leaf * 128 + 128, leaf * 64 : leaf * 64 + 64] = shift[s].T
    return (
        perm,
        perm.T.copy(),
        face,
        face.T.copy(),
        spread,
        shift.reshape(448, 128),
        back.reshape(7 * 512, 256),
    )


def dot(a, b):
    return jnp.dot(a, b, preferred_element_type=F32)


def kernel(
    ids, leaves, cot, w_hbm, perm, permt, face, facet, spread, shift, back,
    out, gl, gw,
    wr, xc, xt, xb, e_int, e5, gcot, cf, t128, e1s, e1r, e2s, e2r, codes, codes_in, codes_sm,
    ghost, gs, gx, gwn, gwp, cbuf, xsa, xsb, xsp, xsm, xs2p, xs2m, xra, xrb, xrp, xrm, xr2p, xr2m,
    own, lsend, lrecv, fs, frecv, of,
    w_sem, sm_sem, e1_ss, e1_rs, id_ss, id_rs, e2_ss, e2_rs, c_ss, c_rs, x_ss, x_rs, l_ss, l_rs, f_ss, f_rs,
):
    ms = lax.axis_index("scene")
    ml = lax.axis_index("leaf")
    my, mz = ml // 8, ml % 8
    mx, mc = ms // 2, ms % 2
    count = ids[3, 0]

    def leaf_at(d):
        return ((my + d // 8) % 4) * 8 + (mz + d % 8) % 8

    def leaf_from(d):
        return ((my + 4 - d // 8) % 4) * 8 + (mz + 8 - d % 8) % 8

    for n, t in enumerate(ORDER):
        pltpu.make_async_copy(
            w_hbm.at[pl.ds(t * 128, 128)], wr.at[pl.ds(n * 128, 128)], w_sem
        ).start()

    barrier = pltpu.get_barrier_semaphore()

    @pl.loop(1, 32)
    def _(d):
        pl.semaphore_signal(barrier, inc=1, device_id=(ms, leaf_at(d)), device_id_type=MESH)

    @pl.loop(1, 8)
    def _(d):
        pl.semaphore_signal(barrier, inc=1, device_id=((ms + d) % 8, ml), device_id_type=MESH)

    @pl.loop(0, 8)
    def _(i):
        rows = pl.ds(pl.multiple_of(i * 64, 64), 64)
        g = jnp.where(i < count, cot[rows, :], jnp.zeros((), BF))
        gcot[rows, :] = g
        cf[pl.ds(i * 8, 8)] = dot(face[...], g).astype(BF).reshape(8, 16, 256)

    lane = lax.broadcasted_iota(jnp.int32, (1, 128), 1)

    @pl.loop(0, 32)
    def _(o):
        row = jnp.zeros((1, 128), jnp.int32)
        for k in range(4):
            e1s[o * 4 + k] = cf[ids[0, o * 4 + k]]
            row = jnp.where((lane & 63) >> 4 == k, ids[1, o * 4 + k], row)
        codes[o] = row

    pl.semaphore_wait(barrier, 38)

    def id_copy(d, to):
        return pltpu.make_async_remote_copy(
            src_ref=codes.at[to], dst_ref=codes_in.at[ml],
            send_sem=id_ss.at[d], recv_sem=id_rs.at[d],
            device_id=(ms, to), device_id_type=MESH,
        )

    def e1_copy(d, to):
        return pltpu.make_async_remote_copy(
            src_ref=e1s.at[pl.ds(to * 4, 4)],
            dst_ref=e1r.at[pl.ds(ml * 4, 4)],
            send_sem=e1_ss.at[d], recv_sem=e1_rs.at[d],
            device_id=(ms, to), device_id_type=MESH,
        )

    def e2_copy(d, to):
        return pltpu.make_async_remote_copy(
            src_ref=e2s.at[pl.ds(to * 4, 4)],
            dst_ref=e2r.at[pl.ds(ml * 4, 4)],
            send_sem=e2_ss.at[d], recv_sem=e2_rs.at[d],
            device_id=(ms, to), device_id_type=MESH,
        )

    @pl.loop(1, 32)
    def _(d):
        id_copy(d, leaf_at(d)).start()

    @pl.loop(1, 32)
    def _(d):
        e1_copy(d, leaf_at(d)).start()

    codes_in[ml] = codes[ml]
    mine = pl.ds(ml * 4, 4)
    e1r[mine] = e1s[mine]

    @pl.loop(0, 8)
    def _(i):
        at = pl.multiple_of(i * 512, 512)
        block = jnp.concatenate([leaves[pl.ds(at, 256), :], leaves[pl.ds(at + 256, 256), :]], axis=1)
        block = jnp.where(i < count, block, jnp.zeros((), BF))
        sorted_ = dot(perm[...], block).astype(BF)
        for h in range(2):
            for p in range(8):
                xc[pl.ds(pl.multiple_of(i * 64, 64) + 32 * h, 32), p * 128 : p * 128 + 128] = sorted_[
                    p * 32 : p * 32 + 32, h * 128 : h * 128 + 128
                ]

    for p in range(8):
        xt[p * 128 : p * 128 + 128, :] = xc[:, p * 128 : p * 128 + 128].T

    pltpu.make_async_copy(w_hbm, wr, w_sem).wait()

    @pl.loop(0, 2)
    def _(b):
        rows = pl.ds(pl.multiple_of(b * 256, 256), 256)
        e_int[rows, :] = dot(xc[rows, :], wr[0:1024, :])

    @pl.loop(0, 2)
    def _(g):
        rows = pl.ds(pl.multiple_of(g * 256, 256), 256)
        for s in range(1, 8):
            ps = HOLD[s]
            for first in range(0, len(ps), 2):
                pair = ps[first : first + 2]
                block = jnp.concatenate([xc[rows, p * 128 : p * 128 + 128] for p in pair], axis=1)
                moved = dot(back[(s - 1) * 512 : s * 512, :], block).astype(BF)
                at = (FIRST[s] - 8 + first) * 128
                xb[pl.ds(pl.multiple_of(g * 512, 512), 512), at : at + 128 * len(pair)] = moved

    @pl.loop(0, 4)
    def _(b):
        rows = pl.ds(pl.multiple_of(b * 256, 256), 256)
        e5[rows, :] = dot(xb[rows, :], wr[1024:3456, :])

    @pl.loop(0, 8)
    def _(i):
        at = pl.multiple_of(i * 128, 128)
        t64 = e5[pl.ds(at + 64, 64), :].astype(BF)
        t128[pl.ds(i * 8, 8)] = dot(spread[...], t64).astype(BF).reshape(8, 16, 256)

    @pl.loop(1, 32)
    def _(d):
        id_copy(d, leaf_at(d)).wait()

    to_sm = pltpu.make_async_copy(codes_in, codes_sm, sm_sem)
    to_sm.start()
    to_sm.wait()

    @pl.loop(0, 32)
    def _(r):
        for k in range(4):
            e2s[r * 4 + k] = t128[codes_sm[r, 0, k * 16]]

    e2r[mine] = e2s[mine]

    @pl.loop(1, 32)
    def _(d):
        e1_copy(d, leaf_at(d)).wait()

    @pl.loop(1, 32)
    def _(d):
        e2_copy(d, leaf_at(d)).start()

    ghost[...] = jnp.zeros_like(ghost)
    goal = lax.broadcasted_iota(jnp.int32, (512, 128), 0)

    @pl.loop(0, 16)
    def _(m):
        row = jnp.where(lane < 64, codes_in[2 * m], codes_in[2 * m + 1])
        d = row & 7
        target = (row >> 3) * 64 + jnp.where(d < 3, 16 * d, 36 + 4 * d) + (lane & 15)
        pick = jnp.where(goal == target, 1.0, 0.0).astype(BF)
        ghost[...] += dot(pick, e1r[pl.ds(m * 8, 8)].reshape(128, 256))

    gs[0:512, :] = gcot[...]

    @pl.loop(0, 8)
    def _(i):
        rows = pl.ds(pl.multiple_of(i * 64, 64), 64)
        g5 = jnp.concatenate([gcot[rows, :], ghost[rows, :].astype(BF)], axis=0)
        moved = dot(shift[...], g5).astype(BF)
        for s in range(1, 8):
            gs[pl.ds(pl.multiple_of(s * 512 + i * 64, 64), 64), :] = moved[(s - 1) * 64 : s * 64, :]

    gwn[3456:3472, :] = jnp.zeros((16, 256), F32)
    for s in SHIFTS:
        for p in HOLD[s]:
            t = tap_of(p, s)
            gwn[t * 128 : t * 128 + 128, :] = dot(
                xt[p * 128 : p * 128 + 128, :], gs[s * 512 : s * 512 + 512, :]
            )

    @pl.loop(0, 16)
    def _(m):
        at = pl.multiple_of(m * 216, 8)
        even = gwn[pl.ds(at, 112), :]
        odd = gwn[pl.ds(pl.multiple_of(at + 104, 8), 120), :][4:116, :]
        for s in range(7):
            gwp[pl.ds(pl.multiple_of(s * 512 + m * 32, 16), 16), :] = even[s * 16 : s * 16 + 16, :]
            gwp[pl.ds(pl.multiple_of(s * 512 + m * 32 + 16, 16), 16), :] = odd[s * 16 : s * 16 + 16, :]

    gwp[7 * 512 : 8 * 512, :] = jnp.zeros((512, 256), F32)

    def c_copy(n):
        cx = (mx + n) % 4
        return pltpu.make_async_remote_copy(
            src_ref=gwp.at[pl.ds(pl.multiple_of((2 * cx + 1 - mc) * 512, 512), 512)],
            dst_ref=cbuf.at[pl.ds(pl.multiple_of(cx * 512, 512), 512)],
            send_sem=c_ss.at[n], recv_sem=c_rs.at[n],
            device_id=(2 * mx + 1 - mc, ml), device_id_type=MESH,
        )

    for n in (2, 1, 3, 0):
        c_copy(n).start()

    def chip_sum(n, half):
        cx = (mx + n) % 4
        a = gwp[pl.ds(pl.multiple_of((2 * cx + mc) * 512 + half * 256, 256), 256), :]
        b = cbuf[pl.ds(pl.multiple_of(cx * 512 + half * 256, 256), 256), :]
        return a + b

    up = (2 * ((mx + 1) % 4) + mc, ml)
    down = (2 * ((mx + 3) % 4) + mc, ml)

    def x_copy(n, src, dst, to):
        return pltpu.make_async_remote_copy(
            src_ref=src, dst_ref=dst, send_sem=x_ss.at[n], recv_sem=x_rs.at[n],
            device_id=to, device_id_type=MESH,
        )

    c_copy(2).wait()
    xsa[...] = chip_sum(2, 0).astype(BF)
    xsb[...] = chip_sum(2, 1).astype(BF)
    x0 = x_copy(0, xsa, xra, up)
    x0.start()
    x1 = x_copy(1, xsb, xrb, down)
    x1.start()
    c_copy(1).wait()
    xsp[...] = chip_sum(1, 1).astype(BF)
    x2 = x_copy(2, xsp, xrp, up)
    x2.start()
    c_copy(3).wait()
    xsm[...] = chip_sum(3, 0).astype(BF)
    x3 = x_copy(3, xsm, xrm, down)
    x3.start()
    c_copy(0).wait()
    x0.wait()
    xs2p[...] = (chip_sum(1, 0) + xra[...].astype(F32)).astype(BF)
    x4 = x_copy(4, xs2p, xr2p, up)
    x4.start()
    x1.wait()
    xs2m[...] = (chip_sum(3, 1) + xrb[...].astype(F32)).astype(BF)
    x5 = x_copy(5, xs2m, xr2m, down)
    x5.start()

    @pl.loop(0, 2)
    def _(b):
        rows = pl.ds(pl.multiple_of(b * 256, 256), 256)
        for s in SHIFTS:
            ps = HOLD[s]
            first = FIRST[s] * 128
            part = lax.dot_general(
                gs[pl.ds(pl.multiple_of(s * 512 + b * 256, 256), 256), :],
                wr[first : first + 128 * len(ps), :],
                (((1,), (1,)), ((), ())),
                preferred_element_type=F32,
            )
            for n, p in enumerate(ps):
                piece = part[:, n * 128 : n * 128 + 128]
                if s == 0:
                    gx[rows, p * 128 : p * 128 + 128] = piece
                else:
                    gx[rows, p * 128 : p * 128 + 128] += piece

    @pl.loop(0, 8)
    def _(i):
        halves = []
        for h in range(2):
            rows = pl.ds(pl.multiple_of(i * 64, 64) + 32 * h, 32)
            halves.append(jnp.concatenate([gx[rows, p * 128 : p * 128 + 128] for p in range(8)], axis=0))
        block = jnp.concatenate(halves, axis=1).astype(BF)
        block = jnp.where(i < count, block, jnp.zeros((), BF))
        back_ = dot(permt[...], block).astype(BF)
        at = pl.multiple_of(i * 512, 512)
        gl[pl.ds(at, 256), :] = back_[:, 0:128]
        gl[pl.ds(at + 256, 256), :] = back_[:, 128:256]

    x3.wait()
    x4.wait()
    own[0:256, :] = chip_sum(0, 0) + xrm[...].astype(F32) + xr2p[...].astype(F32)
    x2.wait()
    x5.wait()
    own[256:512, :] = chip_sum(0, 1) + xrp[...].astype(F32) + xr2m[...].astype(F32)
    lsend[...] = own[...].astype(BF)

    def l_copy(d, to):
        return pltpu.make_async_remote_copy(
            src_ref=lsend.at[pl.ds(pl.multiple_of(to * 16, 16), 16)],
            dst_ref=lrecv.at[pl.ds(pl.multiple_of(ml * 16, 16), 16)],
            send_sem=l_ss.at[d], recv_sem=l_rs.at[d],
            device_id=(ms, to), device_id_type=MESH,
        )

    @pl.loop(1, 32)
    def _(d):
        l_copy(d, leaf_at(d)).start()

    tile = pl.ds(pl.multiple_of(ml * 16, 16), 16)
    lrecv[tile, :] = lsend[tile, :]

    @pl.loop(1, 32)
    def _(d):
        l_copy(d, leaf_at(d)).wait()

    total = jnp.zeros((16, 256), F32)
    for r in range(32):
        total = total + lrecv[r * 16 : r * 16 + 16, :].astype(F32)
    fs[...] = total

    def f_copy(d):
        return pltpu.make_async_remote_copy(
            src_ref=fs, dst_ref=frecv.at[pl.ds(pl.multiple_of(ms * 16, 16), 16)],
            send_sem=f_ss.at[d], recv_sem=f_rs.at[d],
            device_id=((ms + d) % 8, ml), device_id_type=MESH,
        )

    @pl.loop(1, 8)
    def _(d):
        f_copy(d).start()

    frecv[pl.ds(pl.multiple_of(ms * 16, 16), 16), :] = fs[...]

    @pl.loop(1, 32)
    def _(d):
        e2_copy(d, leaf_at(d)).wait()

    @pl.loop(0, 8)
    def _(i):
        for d in range(7):
            of[d * 16 : d * 16 + 16, :] = e2r[ids[2, i * 8 + d]]
        of[112:128, :] = jnp.zeros((16, 256), BF)
        rows = pl.ds(pl.multiple_of(i * 64, 64), 64)
        y = e_int[rows, :] + e5[pl.ds(pl.multiple_of(i * 128, 128), 64), :] + dot(facet[...], of[...])
        out[rows, :] = jnp.where(i < count, y, 0.0).astype(BF)

    @pl.loop(1, 8)
    def _(d):
        f_copy(d).wait()

    gw[...] = frecv[0:108, :]


def request_tables(nbr_owner, nbr_slot, counts):
    pad = ((0, 0), (0, 1))
    pick = np.array([code - 1 for code in CODES])
    owners = jnp.pad(nbr_owner[:, pick], pad, constant_values=32).reshape(64)
    blocks = (jnp.pad(nbr_slot[:, pick], pad) * 8 + jnp.arange(8, dtype=jnp.int32)[None, :]).reshape(64)
    n = jnp.arange(64, dtype=jnp.int32)
    rank = jnp.sum((owners[:, None] == owners[None, :]) & (n[None, :] < n[:, None]), axis=1, dtype=jnp.int32)
    place = owners * 4 + rank
    hit = place[None, :] == jnp.arange(128, dtype=jnp.int32)[:, None]
    source = 7 + jnp.sum(jnp.where(hit, n[None, :] - 7, 0), axis=1, dtype=jnp.int32)
    code = 7 + jnp.sum(jnp.where(hit, blocks[None, :] - 7, 0), axis=1, dtype=jnp.int32)
    places = jnp.pad(place, (0, 64))
    return jnp.stack([source, code, places, jnp.broadcast_to(counts.reshape(1), (128,))])


def per_device(leaves, counts, nbr_owner, nbr_slot, weight, cotangent):
    ids = request_tables(nbr_owner[0], nbr_slot[0], counts)
    consts = [jnp.asarray(t, BF) for t in tables()]
    vmem = pl.BlockSpec(memory_space=pltpu.VMEM)
    sems = pltpu.SemaphoreType.DMA
    V = pltpu.VMEM
    out, gl, gw = pl.pallas_call(
        kernel,
        out_shape=(
            jax.ShapeDtypeStruct((512, 256), BF),
            jax.ShapeDtypeStruct((4096, 128), BF),
            jax.ShapeDtypeStruct((108, 256), F32),
        ),
        in_specs=[pl.BlockSpec(memory_space=pltpu.SMEM), vmem, vmem, pl.BlockSpec(memory_space=pl.ANY)]
        + [vmem] * 7,
        out_specs=(vmem, vmem, vmem),
        scratch_shapes=[
            V((3456, 256), BF), V((512, 1024), BF), V((1024, 512), BF), V((1024, 2432), BF),
            V((512, 256), F32), V((1024, 256), F32), V((512, 256), BF), V((64, 16, 256), BF), V((64, 16, 256), BF),
            *[V((128, 16, 256), BF) for _ in range(4)],
            V((32, 1, 128), jnp.int32), V((32, 1, 128), jnp.int32), pltpu.SMEM((32, 1, 128), jnp.int32),
            V((512, 256), F32), V((4096, 256), BF), V((512, 1024), F32), V((3472, 256), F32),
            V((4096, 256), F32), V((2048, 256), F32),
            *[V((256, 256), BF) for _ in range(12)],
            V((512, 256), F32), V((512, 256), BF), V((512, 256), BF), V((16, 256), F32), V((128, 256), F32),
            V((128, 256), BF),
            sems, sems, sems((32,)), sems((32,)), sems((32,)), sems((32,)), sems((32,)), sems((32,)),
            sems((4,)), sems((4,)), sems((6,)), sems((6,)), sems((32,)), sems((32,)), sems((8,)), sems((8,)),
        ],
        compiler_params=pltpu.CompilerParams(
            collective_id=0, has_side_effects=True, vmem_limit_bytes=56 * 1024 * 1024
        ),
        cost_estimate=pl.CostEstimate(flops=3 * 10**9, bytes_accessed=5 * 10**6, transcendentals=0),
    )(ids, leaves.reshape(4096, 128), cotangent.reshape(512, 256), weight, *consts)
    return (
        out.reshape(1, 8, 4, 4, 4, 256),
        gl.reshape(1, 8, 8, 8, 8, 128),
        gw,
    )


def solution(mesh):
    six = P("scene", "leaf", None, None, None, None)
    return jax.shard_map(
        per_device,
        mesh=mesh,
        in_specs=(six, P("scene", "leaf"), P("scene", "leaf", None), P("scene", "leaf", None), P(), six),
        out_specs=(six, six, P("leaf", None)),
        check_vma=False,
    )
```

```python
import functools

import jax
import jax.numpy as jnp
import numpy as np
from jax import lax
from jax.experimental import pallas as pl
from jax.experimental.pallas import tpu as pltpu
from jax.sharding import PartitionSpec as P

MESH = pl.DeviceIdType.MESH
BF = jnp.bfloat16
F32 = jnp.float32
CODES = (1, 2, 4, 3, 5, 6, 7)
SHIFTS = tuple(range(8))
CHUNK, HALFC = 448, 224
FAR_FIRST = (4, 3, 5, 2, 6, 1, 7, 0)
ROWS, PART = 304, 160
HOLD = {s: [p for p in range(8) if p & s == s] for s in SHIFTS}
FIRST = {}
_at = 0
for _s in SHIFTS:
    FIRST[_s] = _at
    _at += len(HOLD[_s])


def tap_of(parity, shift):
    t = 0
    for axis in range(3):
        if not parity >> axis & 1:
            digit = 1
        elif shift >> axis & 1:
            digit = 0
        else:
            digit = 2
        t = 3 * t + digit
    return t


ORDER = [tap_of(p, s) for s in SHIFTS for p in HOLD[s]]


def base_of(d):
    return 16 * d if d < 3 else 36 + 4 * d


def cells_of(d):
    code = CODES[d]
    ranges = [[None] if code >> axis & 1 else list(range(4)) for axis in range(3)]
    return [(i, j, k) for i in ranges[0] for j in ranges[1] for k in ranges[2]]


def tables():
    perm = np.zeros((256, 256), np.float32)
    for x in range(4):
        for y in range(8):
            for z in range(8):
                p = (x & 1) + 2 * (y & 1) + 4 * (z & 1)
                perm[p * 32 + (x >> 1) * 16 + (y >> 1) * 4 + (z >> 1), x * 64 + y * 8 + z] = 1
    facet = np.zeros((64, 128), np.float32)
    low_cells = [c for c in np.ndindex(4, 4, 4) if 0 in c]
    gather = np.zeros((ROWS, 512), np.float32)
    for leaf in range(8):
        for n, (x, y, z) in enumerate(low_cells):
            gather[leaf * 37 + n, leaf * 64 + 16 * x + 4 * y + z] = 1
    expand = np.zeros((64, 16, 384), np.float32)
    spread = np.zeros((128, 64), np.float32)
    place = {}
    for x in range(4):
        for y in range(4):
            for z in range(4):
                place[(x, y, z)] = 16 * x + 4 * y + z
    for d in range(7):
        for v, cell in enumerate(cells_of(d)):
            low = [0 if c is None else c for c in cell]
            facet[16 * low[0] + 4 * low[1] + low[2], d * 16 + v] = 1
            for leaf in range(8):
                expand[leaf * 8 + d, v, leaf * 37 + low_cells.index(tuple(low))] = 1
            spread[d * 16 + v, base_of(d) + v] = 1
            place[tuple(4 if c is None else c for c in cell)] = 64 + base_of(d) + v
    shift = np.zeros((7, 64, 128), np.float32)
    for s in range(1, 8):
        for x in range(4):
            for y in range(4):
                for z in range(4):
                    goal = (x + (s & 1), y + (s >> 1 & 1), z + (s >> 2 & 1))
                    shift[s - 1, 16 * x + 4 * y + z, place[goal]] = 1
    back = np.zeros((7, 512, 256), np.float32)
    for s in range(7):
        for leaf in range(4):
            back[s, leaf * 128 : leaf * 128 + 128, leaf * 64 : leaf * 64 + 64] = shift[s].T
    return (
        perm,
        perm.T.copy(),
        facet,
        spread,
        gather,
        expand,
        shift.reshape(448, 128),
        back.reshape(7 * 512, 256),
    )


def dot(a, b):
    return jnp.dot(a, b, preferred_element_type=F32)


def kernel(
    ids, idv, leaves_h, cot_h, w_h, perm_h, permt_h, facet_h, spread_h, gather_h, expand_h, shift_h, back_h,
    out_h, gl_h, gw,
    leaves, cot, perm, permt, facet, spread, gather, expand, shift, back, out, gl,
    wr, xc, xt, xb, e_int, e5, gcot, ub, t128, e1s, e1r, e2s, e2m, e2r, codes, codes_sm, pick,
    ghost, gs, gx, gwn, gwp, cbuf, xsa, xsb, xsp, xsm, xs2p, xs2m, xra, xrb, xrp, xrm, xr2p, xr2m,
    own, lsend, lrecv, zsend, zrecv, fs, frecv, of,
    in_sem, w_sem, sm_sem, out_sem, ag_ss, ag_rs, iz_ss, iz_rs, iy_ss, iy_rs, e1_ss, e1_rs, ea_ss, ea_rs, eb_ss, eb_rs,
    c_ss, c_rs, x_ss, x_rs, ly_ss, ly_rs, lz_ss, lz_rs, f_ss, f_rs,
):
    ms = lax.axis_index("scene")
    ml = lax.axis_index("leaf")
    my, mz = ml // 8, ml % 8
    mx, mc = ms // 2, ms % 2
    count = ids[3, 0]

    def remote(src, dst, ss, rs, to):
        return pltpu.make_async_remote_copy(
            src_ref=src, dst_ref=dst, send_sem=ss, recv_sem=rs, device_id=to, device_id_type=MESH
        )

    def at_z(d):
        return (ms, my * 8 + (mz + d) % 8)

    def at_y(d):
        return (ms, (my + d) % 4 * 8 + mz)

    loads = [
        pltpu.make_async_copy(src, dst, in_sem.at[n])
        for n, (src, dst) in enumerate(
            (
                (cot_h, cot), (gather_h, gather), (leaves_h, leaves), (perm_h, perm), (expand_h, expand),
                (back_h, back), (spread_h, spread), (shift_h, shift), (permt_h, permt), (facet_h, facet),
            )
        )
    ]
    for load in loads[:4]:
        load.start()

    for n, t in enumerate(ORDER):
        pltpu.make_async_copy(
            w_h.at[pl.ds(t * 128, 128)], wr.at[pl.ds(n * 128, 128)], w_sem
        ).start()
    for load in loads[4:]:
        load.start()

    barrier = pltpu.get_barrier_semaphore()

    @pl.loop(1, 8)
    def _(d):
        pl.semaphore_signal(barrier, inc=1, device_id=at_z(d), device_id_type=MESH)
        pl.semaphore_signal(barrier, inc=1, device_id=((ms + d) % 8, ml), device_id_type=MESH)

    @pl.loop(1, 4)
    def _(d):
        pl.semaphore_signal(barrier, inc=1, device_id=at_y(d), device_id_type=MESH)

    loads[0].wait()

    @pl.loop(0, 8)
    def _(i):
        rows = pl.ds(pl.multiple_of(i * 64, 64), 64)
        gcot[rows, :] = jnp.where(i < count, cot[rows, :], jnp.zeros((), BF))

    loads[1].wait()
    ub[mz] = dot(gather[...], gcot[...]).astype(BF)
    codes[ml, :, 0:128] = idv[0:1, :]
    codes[ml, :, 128:256] = idv[1:2, :]

    loads[2].wait()
    loads[3].wait()

    @pl.loop(0, 8)
    def _(i):
        at = pl.multiple_of(i * 512, 512)
        block = jnp.concatenate([leaves[pl.ds(at, 256), :], leaves[pl.ds(at + 256, 256), :]], axis=1)
        block = jnp.where(i < count, block, jnp.zeros((), BF))
        sorted_ = dot(perm[...], block).astype(BF)
        for h in range(2):
            for p in range(8):
                xc[pl.ds(pl.multiple_of(i * 64, 64) + 32 * h, 32), p * 128 : p * 128 + 128] = sorted_[
                    p * 32 : p * 32 + 32, h * 128 : h * 128 + 128
                ]

    pl.semaphore_wait(barrier, 17)

    halves = (pl.ds(0, PART), pl.ds(PART, ROWS - PART))

    def ag_copy(way, half, hop):
        origin = (mz + 8 - (hop - 1)) % 8 if way == 0 else (mz + hop - 1) % 8
        block = ub.at[origin, halves[half]]
        n = (way * 2 + half) * 4 + hop - 1
        return remote(block, block, ag_ss.at[n], ag_rs.at[n], at_z(1 if way == 0 else 7))

    def iz_copy(d):
        return remote(codes.at[ml], codes.at[ml], iz_ss.at[d], iz_rs.at[d], at_z(d))

    def iy_copy(d):
        group = codes.at[pl.ds(my * 8, 8)]
        return remote(group, group, iy_ss.at[d], iy_rs.at[d], at_y(d))

    @pl.loop(1, 8)
    def _(d):
        iz_copy(d).start()

    for way in range(2):
        for half in (way, 1 - way):
            ag_copy(way, half, 1).start()

    for p in range(8):
        xt[p * 128 : p * 128 + 128, :] = xc[:, p * 128 : p * 128 + 128].T

    @pl.loop(1, 8)
    def _(d):
        iz_copy(d).wait()

    for d in range(1, 4):
        iy_copy(d).start()
    group = pl.ds(my * 8, 8)
    to_sm = pltpu.make_async_copy(codes.at[group], codes_sm.at[group], sm_sem)
    to_sm.start()
    to_sm.wait()

    for load in loads[4:]:
        load.wait()

    def e1_copy(q, d):
        z = (mz + q) % 8
        to = (my + d) % 4
        return remote(
            e1s.at[pl.ds((z * 4 + to) * 4, 4)], e1r.at[pl.ds((z * 4 + my) * 4, 4)],
            e1_ss.at[q * 4 + d], e1_rs.at[q * 4 + d], at_y(d),
        )

    def serve(q):
        z = (mz + q) % 8
        picks = jnp.concatenate(
            [
                expand[codes_sm[my * 8 + z, 0, (y * 8 + mz) * 4 + k]]
                for y in range(4)
                for k in range(4)
            ],
            axis=0,
        )
        rows = dot(picks[:, 0:ROWS], ub[z]).astype(BF)
        e1s[pl.ds(z * 16, 16)] = rows.reshape(16, 16, 256)
        for d in range(1, 4):
            e1_copy(q, d).start()
        e1r[pl.ds((z * 4 + my) * 4, 4)] = e1s[pl.ds((z * 4 + my) * 4, 4)]

    serve(0)
    pltpu.make_async_copy(w_h, wr, w_sem).wait()

    @pl.loop(0, 2)
    def _(b):
        rows = pl.ds(pl.multiple_of(b * 256, 256), 256)
        e_int[rows, :] = dot(xc[rows, :], wr[0:1024, :])

    def forward_shift(g):
        rows = pl.ds(g * 256, 256)
        for s in range(1, 8):
            ps = HOLD[s]
            for first in range(0, len(ps), 2):
                pair = ps[first : first + 2]
                block = jnp.concatenate([xc[rows, p * 128 : p * 128 + 128] for p in pair], axis=1)
                moved = dot(back[(s - 1) * 512 : s * 512, :], block).astype(BF)
                at = (FIRST[s] - 8 + first) * 128
                xb[pl.ds(g * 512, 512), at : at + 128 * len(pair)] = moved

    def forward_rows(b):
        e5[pl.ds(b * 256, 256), :] = dot(xb[pl.ds(b * 256, 256), :], wr[1024:3456, :])
        for i in (2 * b, 2 * b + 1):
            t64 = e5[pl.ds(i * 128 + 64, 64), :].astype(BF)
            t128[pl.ds(i * 8, 8)] = dot(spread[...], t64).astype(BF).reshape(8, 16, 256)

    def hop_done(way, half, hop):
        ag_copy(way, half, hop).wait()
        if hop < (4 if half == way else 3):
            ag_copy(way, half, hop + 1).start()

    def hop_all(hop):
        for half in (0, 1):
            hop_done(0, half, hop)
            hop_done(1, 1 - half, hop)

    def ea_copy(q, d):
        z = (mz + q) % 8
        to = (my + d) % 4
        return remote(
            e2s.at[pl.ds((to * 8 + z) * 4, 4)], e2m.at[pl.ds((z * 4 + my) * 4, 4)],
            ea_ss.at[q * 4 + d], ea_rs.at[q * 4 + d], at_y(d),
        )

    def eb_copy(d):
        z = (mz + d) % 8
        return remote(
            e2m.at[pl.ds(z * 16, 16)], e2r.at[pl.ds(mz * 16, 16)], eb_ss.at[d], eb_rs.at[d], at_z(d)
        )

    forward_shift(0)
    hop_all(1)
    serve(7)
    serve(1)
    forward_shift(1)
    forward_rows(0)
    hop_all(2)
    serve(6)
    serve(2)
    for d in range(1, 4):
        iy_copy(d).wait()
    all_sm = pltpu.make_async_copy(codes, codes_sm, sm_sem)
    all_sm.start()
    all_sm.wait()
    forward_rows(1)
    forward_rows(2)
    hop_all(3)
    serve(5)
    serve(3)
    forward_rows(3)

    lane = lax.broadcasted_iota(jnp.int32, (1, 256), 1)
    goal = lax.broadcasted_iota(jnp.int32, (512, 256), 0)

    def make_pick(q):
        z = (mz + q) % 8
        row = jnp.zeros((1, 256), jnp.int32)
        for y in range(4):
            for k in range(4):
                row = jnp.where(lane >> 4 == y * 4 + k, codes_sm[y * 8 + z, 0, 128 + ml * 4 + k], row)
        d = row & 7
        target = (row >> 3) * 64 + jnp.where(d < 3, 16 * d, 36 + 4 * d) + (lane & 15)
        pick[q] = jnp.where(goal == target, 1.0, 0.0).astype(BF)

    ag_copy(0, 0, 4).wait()
    ag_copy(1, 1, 4).wait()
    serve(4)

    @pl.loop(0, 32)
    def _(r):
        for k in range(4):
            e2s[r * 4 + k] = t128[codes_sm[r, 0, 128 + ml * 4 + k]]

    for q in FAR_FIRST:
        for d in range(1, 4):
            ea_copy(q, d).start()
    for z in range(8):
        e2m[pl.ds((z * 4 + my) * 4, 4)] = e2s[pl.ds((my * 8 + z) * 4, 4)]

    @pl.loop(0, 8)
    def _(q):
        make_pick(q)

    for q in (0, 7, 1, 6, 2, 5, 3, 4):
        for d in range(1, 4):
            e1_copy(q, d).wait()
        z = (mz + q) % 8
        part = dot(pick[q], e1r[pl.ds(z * 16, 16)].reshape(256, 256))
        if q == 0:
            ghost[...] = part
        else:
            ghost[...] += part

    def forward_on(q):
        for d in range(1, 4):
            ea_copy(q, d).wait()
        if q:
            eb_copy(q).start()

    forward_on(4)
    gs[0:512, :] = gcot[...]

    @pl.loop(0, 8)
    def _(i):
        rows = pl.ds(pl.multiple_of(i * 64, 64), 64)
        g5 = jnp.concatenate([gcot[rows, :], ghost[rows, :].astype(BF)], axis=0)
        moved = dot(shift[...], g5).astype(BF)
        for s in range(1, 8):
            gs[pl.ds(pl.multiple_of(s * 512 + i * 64, 64), 64), :] = moved[(s - 1) * 64 : s * 64, :]

    forward_on(3)
    gwn[3456:3472, :] = jnp.zeros((16, 256), F32)
    for s in SHIFTS:
        for p in HOLD[s]:
            t = tap_of(p, s)
            gwn[t * 128 : t * 128 + 128, :] = dot(
                xt[p * 128 : p * 128 + 128, :], gs[s * 512 : s * 512 + 512, :]
            )

    forward_on(5)

    @pl.loop(0, 16)
    def _(n):
        at = pl.multiple_of(n * 216, 8)
        even = gwn[pl.ds(at, 112), :]
        odd = gwn[pl.ds(pl.multiple_of(at + 104, 8), 120), :][4:116, :]
        for h, block in ((0, even), (1, odd)):
            leaf = 2 * n + h
            for m in range(7):
                goal_at = (leaf + m) % 8 * CHUNK + leaf // 8 * 112 + (6 - m) * 16
                gwp[pl.ds(pl.multiple_of(goal_at, 16), 16), :] = block[m * 16 : m * 16 + 16, :]

    def c_copy(n):
        cx = (mx + n) % 4
        return pltpu.make_async_remote_copy(
            src_ref=gwp.at[pl.ds(pl.multiple_of((2 * cx + 1 - mc) * CHUNK, 16), CHUNK)],
            dst_ref=cbuf.at[pl.ds(pl.multiple_of(cx * CHUNK, 16), CHUNK)],
            send_sem=c_ss.at[n], recv_sem=c_rs.at[n],
            device_id=(2 * mx + 1 - mc, ml), device_id_type=MESH,
        )

    for n in (2, 1, 3, 0):
        c_copy(n).start()

    forward_on(2)

    def chip_sum(n, half):
        cx = (mx + n) % 4
        a = gwp[pl.ds(pl.multiple_of((2 * cx + mc) * CHUNK + half * HALFC, 16), HALFC), :]
        b = cbuf[pl.ds(pl.multiple_of(cx * CHUNK + half * HALFC, 16), HALFC), :]
        return a + b

    up = (2 * ((mx + 1) % 4) + mc, ml)
    down = (2 * ((mx + 3) % 4) + mc, ml)

    def x_copy(n, src, dst, to):
        return pltpu.make_async_remote_copy(
            src_ref=src, dst_ref=dst, send_sem=x_ss.at[n], recv_sem=x_rs.at[n],
            device_id=to, device_id_type=MESH,
        )

    c_copy(2).wait()
    xsa[...] = chip_sum(2, 0).astype(BF)
    xsb[...] = chip_sum(2, 1).astype(BF)
    x0 = x_copy(0, xsa, xra, up)
    x0.start()
    x1 = x_copy(1, xsb, xrb, down)
    x1.start()
    forward_on(6)
    c_copy(1).wait()
    xsp[...] = chip_sum(1, 1).astype(BF)
    x2 = x_copy(2, xsp, xrp, up)
    x2.start()
    c_copy(3).wait()
    xsm[...] = chip_sum(3, 0).astype(BF)
    x3 = x_copy(3, xsm, xrm, down)
    x3.start()
    forward_on(1)
    c_copy(0).wait()
    x0.wait()
    xs2p[...] = (chip_sum(1, 0) + xra[...].astype(F32)).astype(BF)
    x4 = x_copy(4, xs2p, xr2p, up)
    x4.start()
    x1.wait()
    xs2m[...] = (chip_sum(3, 1) + xrb[...].astype(F32)).astype(BF)
    x5 = x_copy(5, xs2m, xr2m, down)
    x5.start()

    forward_on(7)
    forward_on(0)
    e2r[pl.ds(mz * 16, 16)] = e2m[pl.ds(mz * 16, 16)]

    @pl.loop(0, 2)
    def _(b):
        rows = pl.ds(pl.multiple_of(b * 256, 256), 256)
        for s in SHIFTS:
            ps = HOLD[s]
            first = FIRST[s] * 128
            part = lax.dot_general(
                gs[pl.ds(pl.multiple_of(s * 512 + b * 256, 256), 256), :],
                wr[first : first + 128 * len(ps), :],
                (((1,), (1,)), ((), ())),
                preferred_element_type=F32,
            )
            for n, p in enumerate(ps):
                piece = part[:, n * 128 : n * 128 + 128]
                if s == 0:
                    gx[rows, p * 128 : p * 128 + 128] = piece
                else:
                    gx[rows, p * 128 : p * 128 + 128] += piece

    @pl.loop(0, 8)
    def _(i):
        halves = []
        for h in range(2):
            rows = pl.ds(pl.multiple_of(i * 64, 64) + 32 * h, 32)
            halves.append(jnp.concatenate([gx[rows, p * 128 : p * 128 + 128] for p in range(8)], axis=0))
        block = jnp.concatenate(halves, axis=1).astype(BF)
        block = jnp.where(i < count, block, jnp.zeros((), BF))
        back_ = dot(permt[...], block).astype(BF)
        at = pl.multiple_of(i * 512, 512)
        gl[pl.ds(at, 256), :] = back_[:, 0:128]
        gl[pl.ds(at + 256, 256), :] = back_[:, 128:256]

    gl_out = pltpu.make_async_copy(gl, gl_h, out_sem.at[0])
    gl_out.start()

    x3.wait()
    x4.wait()
    own[0:HALFC, :] = chip_sum(0, 0) + xrm[...].astype(F32) + xr2p[...].astype(F32)
    x2.wait()
    x5.wait()
    own[HALFC:CHUNK, :] = chip_sum(0, 1) + xrp[...].astype(F32) + xr2m[...].astype(F32)
    lsend[...] = own[...].astype(BF)

    def ly_copy(d):
        to = (my + d) % 4
        return remote(
            lsend.at[pl.ds(pl.multiple_of(to * 112, 16), 112)],
            lrecv.at[pl.ds(pl.multiple_of(my * 112, 16), 112)],
            ly_ss.at[d], ly_rs.at[d], at_y(d),
        )

    for d in (2, 1, 3):
        ly_copy(d).start()
    total = own[pl.ds(pl.multiple_of(my * 112, 16), 112), :]
    for d in (2, 1, 3):
        ly_copy(d).wait()
        came = (my + 4 - d) % 4
        total = total + lrecv[pl.ds(pl.multiple_of(came * 112, 16), 112), :].astype(F32)
    zsend[0:112, :] = total

    def block_for(z):
        return (z + 14 - ms) % 8

    def lz_copy(d):
        c = block_for((mz + d) % 8)
        return remote(
            zsend.at[pl.ds(pl.multiple_of(c * 16, 16), 16)],
            zrecv.at[pl.ds(pl.multiple_of(mz * 16, 16), 16)],
            lz_ss.at[d], lz_rs.at[d], at_z(d),
        )

    mine = block_for(mz)
    for d in FAR_FIRST[:7]:
        @pl.when(block_for((mz + d) % 8) != 7)
        def _():
            lz_copy(d).start()

    def f_copy(d):
        return remote(
            fs, frecv.at[pl.ds(pl.multiple_of((6 - mine) * 16, 16), 16)],
            f_ss.at[d], f_rs.at[d], ((ms + d) % 8, ml),
        )

    @pl.when(mine != 7)
    def _():
        for d in FAR_FIRST[:7]:
            lz_copy(d).wait_recv()
        total = zsend[pl.ds(pl.multiple_of(mine * 16, 16), 16), :]
        for d in range(1, 8):
            total = total + zrecv[pl.ds(pl.multiple_of((mz + d) % 8 * 16, 16), 16), :]
        fs[...] = total

        @pl.loop(1, 8)
        def _(d):
            f_copy(d).start()

        frecv[pl.ds(pl.multiple_of((6 - mine) * 16, 16), 16), :] = fs[...]

    for d in FAR_FIRST[:7]:
        @pl.when(block_for((mz + d) % 8) != 7)
        def _():
            lz_copy(d).wait_send()

    for d in range(1, 8):
        eb_copy(d).wait()

    @pl.loop(0, 8)
    def _(i):
        for d in range(7):
            of[d * 16 : d * 16 + 16, :] = e2r[ids[2, i * 8 + d]]
        of[112:128, :] = jnp.zeros((16, 256), BF)
        rows = pl.ds(pl.multiple_of(i * 64, 64), 64)
        y = e_int[rows, :] + e5[pl.ds(pl.multiple_of(i * 128, 128), 64), :] + dot(facet[...], of[...])
        out[rows, :] = jnp.where(i < count, y, 0.0).astype(BF)

    out_out = pltpu.make_async_copy(out, out_h, out_sem.at[1])
    out_out.start()

    @pl.loop(1, 8)
    def _(d):
        @pl.when((mz + 14 - (ms + 8 - d) % 8) % 8 != 7)
        def _():
            came = (mz + 14 - (ms + 8 - d) % 8) % 8
            remote(
                fs, frecv.at[pl.ds(pl.multiple_of((6 - came) * 16, 16), 16)],
                f_ss.at[d], f_rs.at[d], ((ms + d) % 8, ml),
            ).wait_recv()

    @pl.when(mine != 7)
    def _():
        @pl.loop(1, 8)
        def _(d):
            f_copy(d).wait_send()

    gw[...] = frecv[0:108, :]
    gl_out.wait()
    out_out.wait()


def request_tables(nbr_owner, nbr_slot, counts):
    pad = ((0, 0), (0, 1))
    pick = np.array([code - 1 for code in CODES])
    owners = jnp.pad(nbr_owner[:, pick], pad, constant_values=32).reshape(64)
    blocks = (jnp.pad(nbr_slot[:, pick], pad) * 8 + jnp.arange(8, dtype=jnp.int32)[None, :]).reshape(64)
    n = jnp.arange(64, dtype=jnp.int32)
    rank = jnp.sum((owners[:, None] == owners[None, :]) & (n[None, :] < n[:, None]), axis=1, dtype=jnp.int32)
    place = owners * 4 + rank
    hit = place[None, :] == jnp.arange(128, dtype=jnp.int32)[:, None]
    source = 7 + jnp.sum(jnp.where(hit, n[None, :] - 7, 0), axis=1, dtype=jnp.int32)
    code = 7 + jnp.sum(jnp.where(hit, blocks[None, :] - 7, 0), axis=1, dtype=jnp.int32)
    places = jnp.pad((owners % 8 * 4 + owners // 8) * 4 + rank, (0, 64))
    return jnp.stack([source, code, places, jnp.broadcast_to(counts.reshape(1), (128,))])


def per_device(leaves, counts, nbr_owner, nbr_slot, weight, cotangent):
    ids = request_tables(nbr_owner[0], nbr_slot[0], counts)
    consts = [jnp.asarray(t, BF) for t in tables()]
    vmem = pl.BlockSpec(memory_space=pltpu.VMEM)
    hbm = pl.BlockSpec(memory_space=pl.ANY)
    sems = pltpu.SemaphoreType.DMA
    V = pltpu.VMEM
    out, gl, gw = pl.pallas_call(
        kernel,
        out_shape=(
            jax.ShapeDtypeStruct((512, 256), BF),
            jax.ShapeDtypeStruct((4096, 128), BF),
            jax.ShapeDtypeStruct((108, 256), F32),
        ),
        in_specs=[pl.BlockSpec(memory_space=pltpu.SMEM), vmem] + [hbm] * 11,
        out_specs=(hbm, hbm, vmem),
        scratch_shapes=[
            V((4096, 128), BF), V((512, 256), BF), *[V(t.shape, BF) for t in consts], V((512, 256), BF), V((4096, 128), BF),
            V((3456, 256), BF), V((512, 1024), BF), V((1024, 512), BF), V((1024, 2432), BF),
            V((512, 256), F32), V((1024, 256), F32), V((512, 256), BF), V((8, ROWS, 256), BF), V((64, 16, 256), BF),
            *[V((128, 16, 256), BF) for _ in range(5)],
            V((32, 1, 256), jnp.int32), pltpu.SMEM((32, 1, 256), jnp.int32), V((8, 512, 256), BF),
            V((512, 256), F32), V((4096, 256), BF), V((512, 1024), F32), V((3472, 256), F32),
            V((8 * CHUNK, 256), F32), V((4 * CHUNK, 256), F32),
            *[V((HALFC, 256), BF) for _ in range(12)],
            V((CHUNK, 256), F32), V((CHUNK, 256), BF), V((CHUNK, 256), BF), V((128, 256), F32), V((128, 256), F32),
            V((16, 256), F32), V((128, 256), F32), V((128, 256), BF),
            sems((10,)), sems, sems, sems((2,)), sems((16,)), sems((16,)), sems((8,)), sems((8,)), sems((4,)), sems((4,)),
            sems((32,)), sems((32,)), sems((32,)), sems((32,)), sems((8,)), sems((8,)),
            sems((4,)), sems((4,)), sems((6,)), sems((6,)), sems((4,)), sems((4,)), sems((8,)), sems((8,)),
            sems((8,)), sems((8,)),
        ],
        compiler_params=pltpu.CompilerParams(
            collective_id=0, has_side_effects=True, vmem_limit_bytes=56 * 1024 * 1024
        ),
        cost_estimate=pl.CostEstimate(flops=3 * 10**9, bytes_accessed=5 * 10**6, transcendentals=0),
    )(ids, ids, leaves.reshape(4096, 128), cotangent.reshape(512, 256), weight, *consts)
    return (
        out.reshape(1, 8, 4, 4, 4, 256),
        gl.reshape(1, 8, 8, 8, 8, 128),
        gw,
    )


def solution(mesh):
    six = P("scene", "leaf", None, None, None, None)
    return jax.shard_map(
        per_device,
        mesh=mesh,
        in_specs=(six, P("scene", "leaf"), P("scene", "leaf", None), P("scene", "leaf", None), P(), six),
        out_specs=(six, six, P("leaf", None)),
        check_vma=False,
    )
```

```python
import functools

import jax
import jax.numpy as jnp
import numpy as np
from jax import lax
from jax.experimental import pallas as pl
from jax.experimental.pallas import tpu as pltpu
from jax.sharding import PartitionSpec as P

MESH = pl.DeviceIdType.MESH
BF = jnp.bfloat16
F32 = jnp.float32
CODES = (1, 2, 4, 3, 5, 6, 7)
SHIFTS = tuple(range(8))
CHUNK, HALFC = 448, 224
FAR_FIRST = (4, 3, 5, 2, 6, 1, 7, 0)
ROWS, PART = 304, 160
HOLD = {s: [p for p in range(8) if p & s == s] for s in SHIFTS}
FIRST = {}
_at = 0
for _s in SHIFTS:
    FIRST[_s] = _at
    _at += len(HOLD[_s])


def tap_of(parity, shift):
    t = 0
    for axis in range(3):
        if not parity >> axis & 1:
            digit = 1
        elif shift >> axis & 1:
            digit = 0
        else:
            digit = 2
        t = 3 * t + digit
    return t


ORDER = [tap_of(p, s) for s in SHIFTS for p in HOLD[s]]


def base_of(d):
    return 16 * d if d < 3 else 36 + 4 * d


def cells_of(d):
    code = CODES[d]
    ranges = [[None] if code >> axis & 1 else list(range(4)) for axis in range(3)]
    return [(i, j, k) for i in ranges[0] for j in ranges[1] for k in ranges[2]]


def tables():
    perm = np.zeros((256, 256), np.float32)
    for x in range(4):
        for y in range(8):
            for z in range(8):
                p = (x & 1) + 2 * (y & 1) + 4 * (z & 1)
                perm[p * 32 + (x >> 1) * 16 + (y >> 1) * 4 + (z >> 1), x * 64 + y * 8 + z] = 1
    facet = np.zeros((64, 128), np.float32)
    low_cells = [c for c in np.ndindex(4, 4, 4) if 0 in c]
    gather = np.zeros((ROWS, 512), np.float32)
    for leaf in range(8):
        for n, (x, y, z) in enumerate(low_cells):
            gather[leaf * 37 + n, leaf * 64 + 16 * x + 4 * y + z] = 1
    expand = np.zeros((64, 16, 384), np.float32)
    spread = np.zeros((128, 64), np.float32)
    place = {}
    for x in range(4):
        for y in range(4):
            for z in range(4):
                place[(x, y, z)] = 16 * x + 4 * y + z
    for d in range(7):
        for v, cell in enumerate(cells_of(d)):
            low = [0 if c is None else c for c in cell]
            facet[16 * low[0] + 4 * low[1] + low[2], d * 16 + v] = 1
            for leaf in range(8):
                expand[leaf * 8 + d, v, leaf * 37 + low_cells.index(tuple(low))] = 1
            spread[d * 16 + v, base_of(d) + v] = 1
            place[tuple(4 if c is None else c for c in cell)] = 64 + base_of(d) + v
    shift = np.zeros((7, 64, 128), np.float32)
    for s in range(1, 8):
        for x in range(4):
            for y in range(4):
                for z in range(4):
                    goal = (x + (s & 1), y + (s >> 1 & 1), z + (s >> 2 & 1))
                    shift[s - 1, 16 * x + 4 * y + z, place[goal]] = 1
    back = np.zeros((7, 512, 256), np.float32)
    for s in range(7):
        for leaf in range(4):
            back[s, leaf * 128 : leaf * 128 + 128, leaf * 64 : leaf * 64 + 64] = shift[s].T
    return (
        perm,
        perm.T.copy(),
        facet,
        spread,
        gather,
        expand,
        shift.reshape(448, 128),
        back.reshape(7 * 512, 256),
    )


def dot(a, b):
    return jnp.dot(a, b, preferred_element_type=F32)


def kernel(
    owners, slots, counts, leaves_h, cot_h, w_h, perm_h, permt_h, facet_h, spread_h, gather_h, expand_h, shift_h, back_h,
    out_h, gl_h, gw,
    leaves, cot, perm, permt, facet, spread, gather, expand, shift, back, out, gl,
    idv, ids, column, blocks, wr, xc, xt, xb, e_int, e5, gcot, ub, t128, e1s, e1r, e2s, e2m, e2r, codes, codes_sm,
    ghost, gs, gx, gwn, gwp, cbuf, xsa, xsb, xsp, xsm, xs2p, xs2m, xra, xrb, xrp, xrm, xr2p, xr2m,
    own, lsend, lrecv, zsend, zrecv, fs, frecv, of,
    in_sem, id_sem, w_sem, sm_sem, out_sem, ag_ss, ag_rs, iz_ss, iz_rs, iy_ss, iy_rs, e1_ss, e1_rs, ea_ss, ea_rs, eb_ss, eb_rs,
    c_ss, c_rs, x_ss, x_rs, ly_ss, ly_rs, lz_ss, lz_rs, f_ss, f_rs,
):
    ms = lax.axis_index("scene")
    ml = lax.axis_index("leaf")
    my, mz = ml // 8, ml % 8
    mx, mc = ms // 2, ms % 2
    count = counts[0, 0]

    def remote(src, dst, ss, rs, to):
        return pltpu.make_async_remote_copy(
            src_ref=src, dst_ref=dst, send_sem=ss, recv_sem=rs, device_id=to, device_id_type=MESH
        )

    def at_z(d):
        return (ms, my * 8 + (mz + d) % 8)

    def at_y(d):
        return (ms, (my + d) % 4 * 8 + mz)

    loads = [
        pltpu.make_async_copy(src, dst, in_sem.at[n])
        for n, (src, dst) in enumerate(
            (
                (cot_h, cot), (gather_h, gather), (leaves_h, leaves), (perm_h, perm), (expand_h, expand),
                (back_h, back), (spread_h, spread), (shift_h, shift), (permt_h, permt), (facet_h, facet),
            )
        )
    ]
    for load in loads[:4]:
        load.start()

    for n, t in enumerate(ORDER):
        pltpu.make_async_copy(
            w_h.at[pl.ds(t * 128, 128)], wr.at[pl.ds(n * 128, 128)], w_sem
        ).start()
    for load in loads[4:]:
        load.start()

    barrier = pltpu.get_barrier_semaphore()

    @pl.loop(1, 8)
    def _(d):
        pl.semaphore_signal(barrier, inc=1, device_id=at_z(d), device_id_type=MESH)
        pl.semaphore_signal(barrier, inc=1, device_id=((ms + d) % 8, ml), device_id_type=MESH)

    @pl.loop(1, 4)
    def _(d):
        pl.semaphore_signal(barrier, inc=1, device_id=at_y(d), device_id_type=MESH)

    for n in range(64):
        i, d = n // 8, n % 8
        if d < 7:
            owner, block = owners[CODES[d] - 1, i], slots[CODES[d] - 1, i] * 8 + d
        else:
            owner, block = jnp.int32(99), jnp.int32(7)
        column[n : n + 1, :] = jnp.full((1, 128), owner, jnp.int32)
        blocks[n : n + 1, :] = jnp.full((1, 128), block, jnp.int32)
    column[64:128, :] = jnp.full((64, 128), 99, jnp.int32)
    blocks[64:128, :] = jnp.full((64, 128), 7, jnp.int32)
    down_n = lax.broadcasted_iota(jnp.int32, (128, 128), 0)
    along_n = lax.broadcasted_iota(jnp.int32, (128, 128), 1)
    owner_down = column[...]
    owner_along = owner_down.T
    same = jnp.where(owner_down == owner_along, 1, 0)
    rank_down = jnp.sum(jnp.where(along_n < down_n, same, 0), axis=1, keepdims=True)
    rank_along = jnp.sum(jnp.where(down_n < along_n, same, 0), axis=0, keepdims=True)
    hit = owner_down * 4 + rank_down == along_n
    own_row = owner_along[0:1, :]
    idv[0:1, :] = 7 + jnp.sum(jnp.where(hit, down_n - 7, 0), axis=0, keepdims=True)
    idv[1:2, :] = 7 + jnp.sum(jnp.where(hit, blocks[...] - 7, 0), axis=0, keepdims=True)
    idv[2:3, :] = ((own_row & 7) * 4 + (own_row >> 3)) * 4 + rank_along
    idv[3:8, :] = jnp.zeros((5, 128), jnp.int32)
    places = pltpu.make_async_copy(idv, ids, id_sem)
    places.start()

    loads[0].wait()

    @pl.loop(0, 8)
    def _(i):
        rows = pl.ds(pl.multiple_of(i * 64, 64), 64)
        gcot[rows, :] = jnp.where(i < count, cot[pl.ds(i * 16, 16)].reshape(64, 256), jnp.zeros((), BF))

    loads[1].wait()
    ub[mz] = dot(gather[...], gcot[...]).astype(BF)
    codes[ml, :, 0:128] = idv[0:1, :]
    codes[ml, :, 128:256] = idv[1:2, :]

    loads[2].wait()
    loads[3].wait()

    @pl.loop(0, 8)
    def _(i):
        at = pl.multiple_of(i * 512, 512)
        block = jnp.concatenate([leaves[pl.ds(at, 256), :], leaves[pl.ds(at + 256, 256), :]], axis=1)
        block = jnp.where(i < count, block, jnp.zeros((), BF))
        sorted_ = dot(perm[...], block).astype(BF)
        for h in range(2):
            for p in range(8):
                xc[pl.ds(pl.multiple_of(i * 64, 64) + 32 * h, 32), p * 128 : p * 128 + 128] = sorted_[
                    p * 32 : p * 32 + 32, h * 128 : h * 128 + 128
                ]

    pl.semaphore_wait(barrier, 17)

    halves = (pl.ds(0, PART), pl.ds(PART, ROWS - PART))

    def ag_copy(way, half, hop):
        origin = (mz + 8 - (hop - 1)) % 8 if way == 0 else (mz + hop - 1) % 8
        block = ub.at[origin, halves[half]]
        n = (way * 2 + half) * 4 + hop - 1
        return remote(block, block, ag_ss.at[n], ag_rs.at[n], at_z(1 if way == 0 else 7))

    def iz_copy(d):
        return remote(codes.at[ml], codes.at[ml], iz_ss.at[d], iz_rs.at[d], at_z(d))

    def iy_copy(d):
        group = codes.at[pl.ds(my * 8, 8)]
        return remote(group, group, iy_ss.at[d], iy_rs.at[d], at_y(d))

    @pl.loop(1, 8)
    def _(d):
        iz_copy(d).start()

    for way in range(2):
        for half in (way, 1 - way):
            ag_copy(way, half, 1).start()

    for p in range(8):
        xt[p * 128 : p * 128 + 128, :] = xc[:, p * 128 : p * 128 + 128].T

    @pl.loop(1, 8)
    def _(d):
        iz_copy(d).wait()

    for d in range(1, 4):
        iy_copy(d).start()
    group = pl.ds(my * 8, 8)
    to_sm = pltpu.make_async_copy(codes.at[group], codes_sm.at[group], sm_sem)
    to_sm.start()
    to_sm.wait()

    for load in loads[4:]:
        load.wait()

    def e1_copy(q, d):
        z = (mz + q) % 8
        to = (my + d) % 4
        return remote(
            e1s.at[pl.ds((z * 4 + to) * 4, 4)], e1r.at[pl.ds((z * 4 + my) * 4, 4)],
            e1_ss.at[q * 4 + d], e1_rs.at[q * 4 + d], at_y(d),
        )

    def serve(q):
        z = (mz + q) % 8
        picks = jnp.concatenate(
            [
                expand[codes_sm[my * 8 + z, 0, (y * 8 + mz) * 4 + k]]
                for y in range(4)
                for k in range(4)
            ],
            axis=0,
        )
        rows = dot(picks[:, 0:ROWS], ub[z]).astype(BF)
        e1s[pl.ds(z * 16, 16)] = rows.reshape(16, 16, 256)
        for d in range(1, 4):
            e1_copy(q, d).start()
        e1r[pl.ds((z * 4 + my) * 4, 4)] = e1s[pl.ds((z * 4 + my) * 4, 4)]

    serve(0)
    pltpu.make_async_copy(w_h, wr, w_sem).wait()

    @pl.loop(0, 2)
    def _(b):
        rows = pl.ds(pl.multiple_of(b * 256, 256), 256)
        e_int[rows, :] = dot(xc[rows, :], wr[0:1024, :])

    def forward_shift(g):
        rows = pl.ds(g * 256, 256)
        for s in range(1, 8):
            ps = HOLD[s]
            for first in range(0, len(ps), 2):
                pair = ps[first : first + 2]
                block = jnp.concatenate([xc[rows, p * 128 : p * 128 + 128] for p in pair], axis=1)
                moved = dot(back[(s - 1) * 512 : s * 512, :], block).astype(BF)
                at = (FIRST[s] - 8 + first) * 128
                xb[pl.ds(g * 512, 512), at : at + 128 * len(pair)] = moved

    def forward_rows(b):
        e5[pl.ds(b * 256, 256), :] = dot(xb[pl.ds(b * 256, 256), :], wr[1024:3456, :])
        for i in (2 * b, 2 * b + 1):
            t64 = e5[pl.ds(i * 128 + 64, 64), :].astype(BF)
            t128[pl.ds(i * 8, 8)] = dot(spread[...], t64).astype(BF).reshape(8, 16, 256)

    def hop_done(way, half, hop):
        ag_copy(way, half, hop).wait()
        if hop < (4 if half == way else 3):
            ag_copy(way, half, hop + 1).start()

    def hop_all(hop):
        for half in (0, 1):
            hop_done(0, half, hop)
            hop_done(1, 1 - half, hop)

    def ea_copy(q, d):
        z = (mz + q) % 8
        to = (my + d) % 4
        return remote(
            e2s.at[pl.ds((to * 8 + z) * 4, 4)], e2m.at[pl.ds((z * 4 + my) * 4, 4)],
            ea_ss.at[q * 4 + d], ea_rs.at[q * 4 + d], at_y(d),
        )

    def eb_copy(d):
        z = (mz + d) % 8
        return remote(
            e2m.at[pl.ds(z * 16, 16)], e2r.at[pl.ds(mz * 16, 16)], eb_ss.at[d], eb_rs.at[d], at_z(d)
        )

    forward_shift(0)
    hop_all(1)
    serve(7)
    serve(1)
    forward_shift(1)
    forward_rows(0)
    hop_all(2)
    serve(6)
    serve(2)
    for d in range(1, 4):
        iy_copy(d).wait()
    all_sm = pltpu.make_async_copy(codes, codes_sm, sm_sem)
    all_sm.start()
    all_sm.wait()
    lane = lax.broadcasted_iota(jnp.int32, (1, 256), 1)
    goal = lax.broadcasted_iota(jnp.int32, (512, 256), 0)

    def gather_ghosts(q):
        z = (mz + q) % 8
        row = jnp.zeros((1, 256), jnp.int32)
        for y in range(4):
            for k in range(4):
                row = jnp.where(lane >> 4 == y * 4 + k, codes_sm[y * 8 + z, 0, 128 + ml * 4 + k], row)
        d = row & 7
        target = (row >> 3) * 64 + jnp.where(d < 3, 16 * d, 36 + 4 * d) + (lane & 15)
        pick = jnp.where(goal == target, 1.0, 0.0).astype(BF)
        for n in range(1, 4):
            e1_copy(q, n).wait()
        part = dot(pick, e1r[pl.ds(z * 16, 16)].reshape(256, 256))
        if q == 0:
            ghost[...] = part
        else:
            ghost[...] += part

    forward_rows(1)
    forward_rows(2)
    forward_rows(3)

    hop_all(3)
    serve(5)
    serve(3)

    @pl.loop(0, 32)
    def _(r):
        for k in range(4):
            e2s[r * 4 + k] = t128[codes_sm[r, 0, 128 + ml * 4 + k]]

    gather_ghosts(0)
    gather_ghosts(7)
    gather_ghosts(1)
    ag_copy(0, 0, 4).wait()
    ag_copy(1, 1, 4).wait()
    serve(4)
    for q in FAR_FIRST:
        for d in range(1, 4):
            ea_copy(q, d).start()
    for z in range(8):
        e2m[pl.ds((z * 4 + my) * 4, 4)] = e2s[pl.ds((my * 8 + z) * 4, 4)]
    for q in (6, 2, 5, 3, 4):
        gather_ghosts(q)

    def forward_on(q):
        for d in range(1, 4):
            ea_copy(q, d).wait()
        if q:
            eb_copy(q).start()

    forward_on(4)
    gs[0:512, :] = gcot[...]

    @pl.loop(0, 8)
    def _(i):
        rows = pl.ds(pl.multiple_of(i * 64, 64), 64)
        g5 = jnp.concatenate([gcot[rows, :], ghost[rows, :].astype(BF)], axis=0)
        moved = dot(shift[...], g5).astype(BF)
        for s in range(1, 8):
            gs[pl.ds(pl.multiple_of(s * 512 + i * 64, 64), 64), :] = moved[(s - 1) * 64 : s * 64, :]

    forward_on(3)
    gwn[3456:3472, :] = jnp.zeros((16, 256), F32)
    for s in SHIFTS:
        for p in HOLD[s]:
            t = tap_of(p, s)
            gwn[t * 128 : t * 128 + 128, :] = dot(
                xt[p * 128 : p * 128 + 128, :], gs[s * 512 : s * 512 + 512, :]
            )

    forward_on(5)

    @pl.loop(0, 16)
    def _(n):
        at = pl.multiple_of(n * 216, 8)
        even = gwn[pl.ds(at, 112), :]
        odd = gwn[pl.ds(pl.multiple_of(at + 104, 8), 120), :][4:116, :]
        for h, block in ((0, even), (1, odd)):
            leaf = 2 * n + h
            for m in range(7):
                goal_at = (leaf + m) % 8 * CHUNK + leaf // 8 * 112 + (6 - m) * 16
                gwp[pl.ds(pl.multiple_of(goal_at, 16), 16), :] = block[m * 16 : m * 16 + 16, :]

    def c_copy(n):
        cx = (mx + n) % 4
        return pltpu.make_async_remote_copy(
            src_ref=gwp.at[pl.ds(pl.multiple_of((2 * cx + 1 - mc) * CHUNK, 16), CHUNK)],
            dst_ref=cbuf.at[pl.ds(pl.multiple_of(cx * CHUNK, 16), CHUNK)],
            send_sem=c_ss.at[n], recv_sem=c_rs.at[n],
            device_id=(2 * mx + 1 - mc, ml), device_id_type=MESH,
        )

    for n in (2, 1, 3, 0):
        c_copy(n).start()

    forward_on(2)

    def chip_sum(n, half):
        cx = (mx + n) % 4
        a = gwp[pl.ds(pl.multiple_of((2 * cx + mc) * CHUNK + half * HALFC, 16), HALFC), :]
        b = cbuf[pl.ds(pl.multiple_of(cx * CHUNK + half * HALFC, 16), HALFC), :]
        return a + b

    up = (2 * ((mx + 1) % 4) + mc, ml)
    down = (2 * ((mx + 3) % 4) + mc, ml)

    def x_copy(n, src, dst, to):
        return pltpu.make_async_remote_copy(
            src_ref=src, dst_ref=dst, send_sem=x_ss.at[n], recv_sem=x_rs.at[n],
            device_id=to, device_id_type=MESH,
        )

    c_copy(2).wait()
    xsa[...] = chip_sum(2, 0).astype(BF)
    xsb[...] = chip_sum(2, 1).astype(BF)
    x0 = x_copy(0, xsa, xra, up)
    x0.start()
    x1 = x_copy(1, xsb, xrb, down)
    x1.start()
    forward_on(6)
    c_copy(1).wait()
    xsp[...] = chip_sum(1, 1).astype(BF)
    x2 = x_copy(2, xsp, xrp, up)
    x2.start()
    c_copy(3).wait()
    xsm[...] = chip_sum(3, 0).astype(BF)
    x3 = x_copy(3, xsm, xrm, down)
    x3.start()
    forward_on(1)
    c_copy(0).wait()
    x0.wait()
    xs2p[...] = (chip_sum(1, 0) + xra[...].astype(F32)).astype(BF)
    x4 = x_copy(4, xs2p, xr2p, up)
    x4.start()
    x1.wait()
    xs2m[...] = (chip_sum(3, 1) + xrb[...].astype(F32)).astype(BF)
    x5 = x_copy(5, xs2m, xr2m, down)
    x5.start()

    forward_on(7)
    forward_on(0)
    e2r[pl.ds(mz * 16, 16)] = e2m[pl.ds(mz * 16, 16)]

    @pl.loop(0, 2)
    def _(b):
        rows = pl.ds(pl.multiple_of(b * 256, 256), 256)
        for s in SHIFTS:
            ps = HOLD[s]
            first = FIRST[s] * 128
            part = lax.dot_general(
                gs[pl.ds(pl.multiple_of(s * 512 + b * 256, 256), 256), :],
                wr[first : first + 128 * len(ps), :],
                (((1,), (1,)), ((), ())),
                preferred_element_type=F32,
            )
            for n, p in enumerate(ps):
                piece = part[:, n * 128 : n * 128 + 128]
                if s == 0:
                    gx[rows, p * 128 : p * 128 + 128] = piece
                else:
                    gx[rows, p * 128 : p * 128 + 128] += piece

    @pl.loop(0, 8)
    def _(i):
        halves = []
        for h in range(2):
            rows = pl.ds(pl.multiple_of(i * 64, 64) + 32 * h, 32)
            halves.append(jnp.concatenate([gx[rows, p * 128 : p * 128 + 128] for p in range(8)], axis=0))
        block = jnp.concatenate(halves, axis=1).astype(BF)
        block = jnp.where(i < count, block, jnp.zeros((), BF))
        back_ = dot(permt[...], block).astype(BF)
        at = pl.multiple_of(i * 512, 512)
        gl[pl.ds(at, 256), :] = back_[:, 0:128]
        gl[pl.ds(at + 256, 256), :] = back_[:, 128:256]

    gl_out = pltpu.make_async_copy(gl, gl_h, out_sem.at[0])
    gl_out.start()

    x3.wait()
    x4.wait()
    own[0:HALFC, :] = chip_sum(0, 0) + xrm[...].astype(F32) + xr2p[...].astype(F32)
    x2.wait()
    x5.wait()
    own[HALFC:CHUNK, :] = chip_sum(0, 1) + xrp[...].astype(F32) + xr2m[...].astype(F32)
    lsend[...] = own[...].astype(BF)

    def ly_copy(d):
        to = (my + d) % 4
        return remote(
            lsend.at[pl.ds(pl.multiple_of(to * 112, 16), 112)],
            lrecv.at[pl.ds(pl.multiple_of(my * 112, 16), 112)],
            ly_ss.at[d], ly_rs.at[d], at_y(d),
        )

    for d in (2, 1, 3):
        ly_copy(d).start()
    total = own[pl.ds(pl.multiple_of(my * 112, 16), 112), :]
    for d in (2, 1, 3):
        ly_copy(d).wait()
        came = (my + 4 - d) % 4
        total = total + lrecv[pl.ds(pl.multiple_of(came * 112, 16), 112), :].astype(F32)
    zsend[0:112, :] = total

    def block_for(z):
        return (z + 14 - ms) % 8

    def lz_copy(d):
        c = block_for((mz + d) % 8)
        return remote(
            zsend.at[pl.ds(pl.multiple_of(c * 16, 16), 16)],
            zrecv.at[pl.ds(pl.multiple_of(mz * 16, 16), 16)],
            lz_ss.at[d], lz_rs.at[d], at_z(d),
        )

    mine = block_for(mz)
    for d in FAR_FIRST[:7]:
        @pl.when(block_for((mz + d) % 8) != 7)
        def _():
            lz_copy(d).start()

    def f_copy(d):
        return remote(
            fs, frecv.at[pl.ds(pl.multiple_of((6 - mine) * 16, 16), 16)],
            f_ss.at[d], f_rs.at[d], ((ms + d) % 8, ml),
        )

    @pl.when(mine != 7)
    def _():
        for d in FAR_FIRST[:7]:
            lz_copy(d).wait_recv()
        total = zsend[pl.ds(pl.multiple_of(mine * 16, 16), 16), :]
        for d in range(1, 8):
            total = total + zrecv[pl.ds(pl.multiple_of((mz + d) % 8 * 16, 16), 16), :]
        fs[...] = total

        @pl.loop(1, 8)
        def _(d):
            f_copy(d).start()

        frecv[pl.ds(pl.multiple_of((6 - mine) * 16, 16), 16), :] = fs[...]

    for d in FAR_FIRST[:7]:
        @pl.when(block_for((mz + d) % 8) != 7)
        def _():
            lz_copy(d).wait_send()

    places.wait()
    for d in range(1, 8):
        eb_copy(d).wait()

    @pl.loop(0, 8)
    def _(i):
        for d in range(7):
            of[d * 16 : d * 16 + 16, :] = e2r[ids[2, i * 8 + d]]
        of[112:128, :] = jnp.zeros((16, 256), BF)
        rows = pl.ds(pl.multiple_of(i * 64, 64), 64)
        y = e_int[rows, :] + e5[pl.ds(pl.multiple_of(i * 128, 128), 64), :] + dot(facet[...], of[...])
        out[pl.ds(i * 16, 16)] = jnp.where(i < count, y, 0.0).astype(BF).reshape(16, 4, 256)

    out_out = pltpu.make_async_copy(out, out_h, out_sem.at[1])
    out_out.start()

    @pl.loop(1, 8)
    def _(d):
        @pl.when((mz + 14 - (ms + 8 - d) % 8) % 8 != 7)
        def _():
            came = (mz + 14 - (ms + 8 - d) % 8) % 8
            remote(
                fs, frecv.at[pl.ds(pl.multiple_of((6 - came) * 16, 16), 16)],
                f_ss.at[d], f_rs.at[d], ((ms + d) % 8, ml),
            ).wait_recv()

    @pl.when(mine != 7)
    def _():
        @pl.loop(1, 8)
        def _(d):
            f_copy(d).wait_send()

    gw[...] = frecv[0:108, :]
    gl_out.wait()
    out_out.wait()


def hand_over(*arrays):
    def copy(*refs):
        n = len(arrays)
        held, sem_in, sem_out = refs[2 * n : 3 * n], refs[3 * n], refs[3 * n + 1]
        into = [pltpu.make_async_copy(refs[k], held[k], sem_in.at[k]) for k in range(n)]
        onto = [pltpu.make_async_copy(held[k], refs[n + k], sem_out.at[k]) for k in range(n)]
        for one in into:
            one.start()
        for one, two in zip(into, onto):
            one.wait()
            two.start()
        for two in onto:
            two.wait()

    hbm = pl.BlockSpec(memory_space=pl.ANY)
    sems = pltpu.SemaphoreType.DMA
    return pl.pallas_call(
        copy,
        out_shape=tuple(jax.ShapeDtypeStruct(a.shape, a.dtype) for a in arrays),
        in_specs=[hbm] * len(arrays),
        out_specs=(hbm,) * len(arrays),
        scratch_shapes=[pltpu.VMEM(a.shape, a.dtype) for a in arrays] + [sems((len(arrays),)), sems((len(arrays),))],
    )(*arrays)


def per_device(leaves, counts, nbr_owner, nbr_slot, weight, cotangent):
    consts = [jnp.asarray(t, BF) for t in tables()]
    vmem = pl.BlockSpec(memory_space=pltpu.VMEM)
    hbm = pl.BlockSpec(memory_space=pl.ANY)
    sems = pltpu.SemaphoreType.DMA
    V = pltpu.VMEM
    out, gl, gw = pl.pallas_call(
        kernel,
        out_shape=(
            jax.ShapeDtypeStruct((128, 4, 256), BF),
            jax.ShapeDtypeStruct((4096, 128), BF),
            jax.ShapeDtypeStruct((108, 256), F32),
        ),
        in_specs=[pl.BlockSpec(memory_space=pltpu.SMEM)] * 3 + [hbm] * 11,
        out_specs=(hbm, hbm, vmem),
        scratch_shapes=[
            V((4096, 128), BF), V((128, 4, 256), BF), *[V(t.shape, BF) for t in consts], V((128, 4, 256), BF), V((4096, 128), BF),
            V((8, 128), jnp.int32), pltpu.SMEM((8, 128), jnp.int32), V((128, 128), jnp.int32), V((128, 128), jnp.int32),
            V((3456, 256), BF), V((512, 1024), BF), V((1024, 512), BF), V((1024, 2432), BF),
            V((512, 256), F32), V((1024, 256), F32), V((512, 256), BF), V((8, ROWS, 256), BF), V((64, 16, 256), BF),
            *[V((128, 16, 256), BF) for _ in range(5)],
            V((32, 1, 256), jnp.int32), pltpu.SMEM((32, 1, 256), jnp.int32),
            V((512, 256), F32), V((4096, 256), BF), V((512, 1024), F32), V((3472, 256), F32),
            V((8 * CHUNK, 256), F32), V((4 * CHUNK, 256), F32),
            *[V((HALFC, 256), BF) for _ in range(12)],
            V((CHUNK, 256), F32), V((CHUNK, 256), BF), V((CHUNK, 256), BF), V((128, 256), F32), V((128, 256), F32),
            V((16, 256), F32), V((128, 256), F32), V((128, 256), BF),
            sems((10,)), sems, sems, sems, sems((2,)), sems((16,)), sems((16,)), sems((8,)), sems((8,)), sems((4,)), sems((4,)),
            sems((32,)), sems((32,)), sems((32,)), sems((32,)), sems((8,)), sems((8,)),
            sems((4,)), sems((4,)), sems((6,)), sems((6,)), sems((4,)), sems((4,)), sems((8,)), sems((8,)),
            sems((8,)), sems((8,)),
        ],
        compiler_params=pltpu.CompilerParams(
            collective_id=0, has_side_effects=True, vmem_limit_bytes=56 * 1024 * 1024
        ),
        cost_estimate=pl.CostEstimate(flops=3 * 10**9, bytes_accessed=5 * 10**6, transcendentals=0),
    )(nbr_owner[0].T, nbr_slot[0].T, counts, leaves.reshape(4096, 128), cotangent.reshape(128, 4, 256), weight, *consts)
    out, gl, gw = hand_over(out, gl, gw)
    return (
        out.reshape(1, 8, 4, 4, 4, 256),
        gl.reshape(1, 8, 8, 8, 8, 128),
        gw,
    )


def solution(mesh):
    six = P("scene", "leaf", None, None, None, None)
    return jax.shard_map(
        per_device,
        mesh=mesh,
        in_specs=(six, P("scene", "leaf"), P("scene", "leaf", None), P("scene", "leaf", None), P(), six),
        out_specs=(six, six, P("leaf", None)),
        check_vma=False,
    )
```

```python
import functools

import jax
import jax.numpy as jnp
import numpy as np
from jax import lax
from jax.experimental import pallas as pl
from jax.experimental.pallas import tpu as pltpu
from jax.sharding import PartitionSpec as P

MESH = pl.DeviceIdType.MESH
BF = jnp.bfloat16
F32 = jnp.float32
CODES = (1, 2, 4, 3, 5, 6, 7)
SHIFTS = tuple(range(8))
CHUNK, HALFC = 448, 224
FAR_FIRST = (4, 3, 5, 2, 6, 1, 7, 0)
ROWS, PART = 304, 160
HOLD = {s: [p for p in range(8) if p & s == s] for s in SHIFTS}
FIRST = {}
_at = 0
for _s in SHIFTS:
    FIRST[_s] = _at
    _at += len(HOLD[_s])


def tap_of(parity, shift):
    t = 0
    for axis in range(3):
        if not parity >> axis & 1:
            digit = 1
        elif shift >> axis & 1:
            digit = 0
        else:
            digit = 2
        t = 3 * t + digit
    return t


ORDER = [tap_of(p, s) for s in SHIFTS for p in HOLD[s]]


def base_of(d):
    return 16 * d if d < 3 else 36 + 4 * d


def cells_of(d):
    code = CODES[d]
    ranges = [[None] if code >> axis & 1 else list(range(4)) for axis in range(3)]
    return [(i, j, k) for i in ranges[0] for j in ranges[1] for k in ranges[2]]


def tables():
    perm = np.zeros((256, 256), np.float32)
    for x in range(4):
        for y in range(8):
            for z in range(8):
                p = (x & 1) + 2 * (y & 1) + 4 * (z & 1)
                perm[p * 32 + (x >> 1) * 16 + (y >> 1) * 4 + (z >> 1), x * 64 + y * 8 + z] = 1
    facet = np.zeros((64, 128), np.float32)
    low_cells = [c for c in np.ndindex(4, 4, 4) if 0 in c]
    gather = np.zeros((ROWS, 512), np.float32)
    for leaf in range(8):
        for n, (x, y, z) in enumerate(low_cells):
            gather[leaf * 37 + n, leaf * 64 + 16 * x + 4 * y + z] = 1
    expand = np.zeros((64, 16, 384), np.float32)
    spread = np.zeros((128, 64), np.float32)
    place = {}
    for x in range(4):
        for y in range(4):
            for z in range(4):
                place[(x, y, z)] = 16 * x + 4 * y + z
    for d in range(7):
        for v, cell in enumerate(cells_of(d)):
            low = [0 if c is None else c for c in cell]
            facet[16 * low[0] + 4 * low[1] + low[2], d * 16 + v] = 1
            for leaf in range(8):
                expand[leaf * 8 + d, v, leaf * 37 + low_cells.index(tuple(low))] = 1
            spread[d * 16 + v, base_of(d) + v] = 1
            place[tuple(4 if c is None else c for c in cell)] = 64 + base_of(d) + v
    shift = np.zeros((7, 64, 128), np.float32)
    for s in range(1, 8):
        for x in range(4):
            for y in range(4):
                for z in range(4):
                    goal = (x + (s & 1), y + (s >> 1 & 1), z + (s >> 2 & 1))
                    shift[s - 1, 16 * x + 4 * y + z, place[goal]] = 1
    back = np.zeros((7, 512, 256), np.float32)
    for s in range(7):
        for leaf in range(4):
            back[s, leaf * 128 : leaf * 128 + 128, leaf * 64 : leaf * 64 + 64] = shift[s].T
    return (
        perm,
        perm.T.copy(),
        facet,
        spread,
        gather,
        expand,
        shift.reshape(448, 128),
        back.reshape(7 * 512, 256),
    )


def dot(a, b):
    return jnp.dot(a, b, preferred_element_type=F32)


def kernel(
    owners, slots, counts, leaves_h, cot_h, w_h, perm_h, permt_h, facet_h, spread_h, gather_h, expand_h, shift_h, back_h,
    out_h, gl_h, gw,
    leaves, cot, perm, permt, facet, spread, gather, expand, shift, back, out, gl,
    idv, ids, column, blocks, wr, xc, xt, xb, e_int, e5, gcot, ub, t128, e1s, e1r, e2s, e2m, e2r, codes, codes_sm,
    ghost, gs, gx, gwn, gwp, cbuf, xsa, xsb, xsp, xsm, xs2p, xs2m, xra, xrb, xrp, xrm, xr2p, xr2m,
    own, lsend, lrecv, zsend, zrecv, fs, frecv, of,
    in_sem, id_sem, w_sem, sm_sem, out_sem, ag_ss, ag_rs, iz_ss, iz_rs, iy_ss, iy_rs, e1_ss, e1_rs, ea_ss, ea_rs, eb_ss, eb_rs,
    c_ss, c_rs, x_ss, x_rs, ly_ss, ly_rs, lz_ss, lz_rs, f_ss, f_rs,
):
    ms = lax.axis_index("scene")
    ml = lax.axis_index("leaf")
    my, mz = ml // 8, ml % 8
    mx, mc = ms // 2, ms % 2
    count = counts[0, 0]

    def remote(src, dst, ss, rs, to):
        return pltpu.make_async_remote_copy(
            src_ref=src, dst_ref=dst, send_sem=ss, recv_sem=rs, device_id=to, device_id_type=MESH
        )

    def at_z(d):
        return (ms, my * 8 + (mz + d) % 8)

    def at_y(d):
        return (ms, (my + d) % 4 * 8 + mz)

    loads = [
        pltpu.make_async_copy(src, dst, in_sem.at[n])
        for n, (src, dst) in enumerate(
            (
                (cot_h, cot), (gather_h, gather), (leaves_h, leaves), (perm_h, perm), (expand_h, expand),
                (back_h, back), (spread_h, spread), (shift_h, shift), (permt_h, permt), (facet_h, facet),
            )
        )
    ]
    for load in loads[:4]:
        load.start()

    for n, t in enumerate(ORDER):
        pltpu.make_async_copy(
            w_h.at[pl.ds(t * 128, 128)], wr.at[pl.ds(n * 128, 128)], w_sem
        ).start()
    for load in loads[4:]:
        load.start()

    barrier = pltpu.get_barrier_semaphore()

    @pl.loop(1, 8)
    def _(d):
        pl.semaphore_signal(barrier, inc=1, device_id=at_z(d), device_id_type=MESH)
        pl.semaphore_signal(barrier, inc=1, device_id=((ms + d) % 8, ml), device_id_type=MESH)

    @pl.loop(1, 4)
    def _(d):
        pl.semaphore_signal(barrier, inc=1, device_id=at_y(d), device_id_type=MESH)

    loads[0].wait()

    @pl.loop(0, 8)
    def _(i):
        rows = pl.ds(pl.multiple_of(i * 64, 64), 64)
        gcot[rows, :] = jnp.where(i < count, cot[pl.ds(i * 16, 16)].reshape(64, 256), jnp.zeros((), BF))

    loads[1].wait()
    ub[mz] = dot(gather[...], gcot[...]).astype(BF)
    pl.semaphore_wait(barrier, 17)

    halves = (pl.ds(0, PART), pl.ds(PART, ROWS - PART))

    def ag_copy(way, half, hop):
        origin = (mz + 8 - (hop - 1)) % 8 if way == 0 else (mz + hop - 1) % 8
        block = ub.at[origin, halves[half]]
        n = (way * 2 + half) * 4 + hop - 1
        return remote(block, block, ag_ss.at[n], ag_rs.at[n], at_z(1 if way == 0 else 7))

    def iz_copy(d):
        return remote(codes.at[ml], codes.at[ml], iz_ss.at[d], iz_rs.at[d], at_z(d))

    def iy_copy(d):
        group = codes.at[pl.ds(my * 8, 8)]
        return remote(group, group, iy_ss.at[d], iy_rs.at[d], at_y(d))

    for way in range(2):
        for half in (way, 1 - way):
            ag_copy(way, half, 1).start()

    for n in range(64):
        i, d = n // 8, n % 8
        if d < 7:
            owner, block = owners[CODES[d] - 1, i], slots[CODES[d] - 1, i] * 8 + d
        else:
            owner, block = jnp.int32(99), jnp.int32(7)
        column[n : n + 1, :] = jnp.full((1, 128), owner, jnp.int32)
        blocks[n : n + 1, :] = jnp.full((1, 128), block, jnp.int32)
    column[64:128, :] = jnp.full((64, 128), 99, jnp.int32)
    blocks[64:128, :] = jnp.full((64, 128), 7, jnp.int32)
    down_n = lax.broadcasted_iota(jnp.int32, (128, 128), 0)
    along_n = lax.broadcasted_iota(jnp.int32, (128, 128), 1)
    owner_down = column[...]
    owner_along = owner_down.T
    same = jnp.where(owner_down == owner_along, 1, 0)
    rank_down = jnp.sum(jnp.where(along_n < down_n, same, 0), axis=1, keepdims=True)
    rank_along = jnp.sum(jnp.where(down_n < along_n, same, 0), axis=0, keepdims=True)
    hit = owner_down * 4 + rank_down == along_n
    own_row = owner_along[0:1, :]
    idv[0:1, :] = 7 + jnp.sum(jnp.where(hit, down_n - 7, 0), axis=0, keepdims=True)
    idv[1:2, :] = 7 + jnp.sum(jnp.where(hit, blocks[...] - 7, 0), axis=0, keepdims=True)
    idv[2:3, :] = ((own_row & 7) * 4 + (own_row >> 3)) * 4 + rank_along
    idv[3:8, :] = jnp.zeros((5, 128), jnp.int32)
    places = pltpu.make_async_copy(idv, ids, id_sem)
    places.start()

    codes[ml, :, 0:128] = idv[0:1, :]
    codes[ml, :, 128:256] = idv[1:2, :]

    @pl.loop(1, 8)
    def _(d):
        iz_copy(d).start()

    def hop_done(way, half, hop):
        ag_copy(way, half, hop).wait()
        if hop < (4 if half == way else 3):
            ag_copy(way, half, hop + 1).start()

    def hop_part(part, hop):
        hop_done(0, part, hop)
        hop_done(1, 1 - part, hop)

    hop_part(0, 1)
    loads[2].wait()
    loads[3].wait()

    @pl.loop(0, 8)
    def _(i):
        at = pl.multiple_of(i * 512, 512)
        block = jnp.concatenate([leaves[pl.ds(at, 256), :], leaves[pl.ds(at + 256, 256), :]], axis=1)
        block = jnp.where(i < count, block, jnp.zeros((), BF))
        sorted_ = dot(perm[...], block).astype(BF)
        for h in range(2):
            for p in range(8):
                xc[pl.ds(pl.multiple_of(i * 64, 64) + 32 * h, 32), p * 128 : p * 128 + 128] = sorted_[
                    p * 32 : p * 32 + 32, h * 128 : h * 128 + 128
                ]

    hop_part(1, 1)
    for p in range(8):
        xt[p * 128 : p * 128 + 128, :] = xc[:, p * 128 : p * 128 + 128].T

    @pl.loop(1, 8)
    def _(d):
        iz_copy(d).wait()

    for d in range(1, 4):
        iy_copy(d).start()
    group = pl.ds(my * 8, 8)
    to_sm = pltpu.make_async_copy(codes.at[group], codes_sm.at[group], sm_sem)
    to_sm.start()

    for load in loads[4:]:
        load.wait()

    def e1_copy(q, d):
        z = (mz + q) % 8
        to = (my + d) % 4
        return remote(
            e1s.at[pl.ds((z * 4 + to) * 4, 4)], e1r.at[pl.ds((z * 4 + my) * 4, 4)],
            e1_ss.at[q * 4 + d], e1_rs.at[q * 4 + d], at_y(d),
        )

    def serve(q):
        z = (mz + q) % 8
        picks = jnp.concatenate(
            [
                expand[codes_sm[my * 8 + z, 0, (y * 8 + mz) * 4 + k]]
                for y in range(4)
                for k in range(4)
            ],
            axis=0,
        )
        rows = dot(picks[:, 0:ROWS], ub[z]).astype(BF)
        e1s[pl.ds(z * 16, 16)] = rows.reshape(16, 16, 256)
        for d in range(1, 4):
            e1_copy(q, d).start()
        e1r[pl.ds((z * 4 + my) * 4, 4)] = e1s[pl.ds((z * 4 + my) * 4, 4)]

    def forward_shift(g):
        rows = pl.ds(g * 256, 256)
        for s in range(1, 8):
            ps = HOLD[s]
            for first in range(0, len(ps), 2):
                pair = ps[first : first + 2]
                block = jnp.concatenate([xc[rows, p * 128 : p * 128 + 128] for p in pair], axis=1)
                moved = dot(back[(s - 1) * 512 : s * 512, :], block).astype(BF)
                at = (FIRST[s] - 8 + first) * 128
                xb[pl.ds(g * 512, 512), at : at + 128 * len(pair)] = moved

    def forward_rows(b):
        e5[pl.ds(b * 256, 256), :] = dot(xb[pl.ds(b * 256, 256), :], wr[1024:3456, :])
        for i in (2 * b, 2 * b + 1):
            t64 = e5[pl.ds(i * 128 + 64, 64), :].astype(BF)
            t128[pl.ds(i * 8, 8)] = dot(spread[...], t64).astype(BF).reshape(8, 16, 256)

    def ea_copy(q, d):
        z = (mz + q) % 8
        to = (my + d) % 4
        return remote(
            e2s.at[pl.ds((to * 8 + z) * 4, 4)], e2m.at[pl.ds((z * 4 + my) * 4, 4)],
            ea_ss.at[q * 4 + d], ea_rs.at[q * 4 + d], at_y(d),
        )

    def eb_copy(d):
        z = (mz + d) % 8
        return remote(
            e2m.at[pl.ds(z * 16, 16)], e2r.at[pl.ds(mz * 16, 16)], eb_ss.at[d], eb_rs.at[d], at_z(d)
        )

    lane = lax.broadcasted_iota(jnp.int32, (1, 256), 1)
    goal = lax.broadcasted_iota(jnp.int32, (512, 256), 0)

    def gather_ghosts(q):
        z = (mz + q) % 8
        row = jnp.zeros((1, 256), jnp.int32)
        for y in range(4):
            for k in range(4):
                row = jnp.where(lane >> 4 == y * 4 + k, codes_sm[y * 8 + z, 0, 128 + ml * 4 + k], row)
        d = row & 7
        target = (row >> 3) * 64 + jnp.where(d < 3, 16 * d, 36 + 4 * d) + (lane & 15)
        pick = jnp.where(goal == target, 1.0, 0.0).astype(BF)
        for n in range(1, 4):
            e1_copy(q, n).wait()
        part = dot(pick, e1r[pl.ds(z * 16, 16)].reshape(256, 256))
        if q == 0:
            ghost[...] = part
        else:
            ghost[...] += part

    hop_part(0, 2)
    to_sm.wait()
    serve(0)
    hop_part(1, 2)
    serve(7)
    serve(1)
    hop_part(0, 3)
    for d in range(1, 4):
        iy_copy(d).wait()
    all_sm = pltpu.make_async_copy(codes, codes_sm, sm_sem)
    all_sm.start()
    pltpu.make_async_copy(w_h, wr, w_sem).wait()
    forward_shift(0)
    hop_part(1, 3)
    all_sm.wait()
    serve(6)
    serve(2)
    serve(5)
    serve(3)
    forward_shift(1)
    ag_copy(0, 0, 4).wait()
    ag_copy(1, 1, 4).wait()
    serve(4)
    forward_rows(0)
    forward_rows(1)
    forward_rows(2)
    forward_rows(3)

    @pl.loop(0, 32)
    def _(r):
        for k in range(4):
            e2s[r * 4 + k] = t128[codes_sm[r, 0, 128 + ml * 4 + k]]

    for q in FAR_FIRST:
        for d in range(1, 4):
            ea_copy(q, d).start()
    for z in range(8):
        e2m[pl.ds((z * 4 + my) * 4, 4)] = e2s[pl.ds((my * 8 + z) * 4, 4)]
    for q in (0, 7, 1, 6, 2, 5, 3, 4):
        gather_ghosts(q)

    def forward_on(q):
        for d in range(1, 4):
            ea_copy(q, d).wait()
        if q:
            eb_copy(q).start()

    forward_on(4)
    gs[0:512, :] = gcot[...]

    @pl.loop(0, 8)
    def _(i):
        rows = pl.ds(pl.multiple_of(i * 64, 64), 64)
        g5 = jnp.concatenate([gcot[rows, :], ghost[rows, :].astype(BF)], axis=0)
        moved = dot(shift[...], g5).astype(BF)
        for s in range(1, 8):
            gs[pl.ds(pl.multiple_of(s * 512 + i * 64, 64), 64), :] = moved[(s - 1) * 64 : s * 64, :]

    forward_on(3)
    gwn[3456:3472, :] = jnp.zeros((16, 256), F32)
    for s in SHIFTS:
        for p in HOLD[s]:
            t = tap_of(p, s)
            gwn[t * 128 : t * 128 + 128, :] = dot(
                xt[p * 128 : p * 128 + 128, :], gs[s * 512 : s * 512 + 512, :]
            )

    forward_on(5)

    @pl.loop(0, 16)
    def _(n):
        at = pl.multiple_of(n * 216, 8)
        even = gwn[pl.ds(at, 112), :]
        odd = gwn[pl.ds(pl.multiple_of(at + 104, 8), 120), :][4:116, :]
        for h, block in ((0, even), (1, odd)):
            leaf = 2 * n + h
            for m in range(7):
                goal_at = (leaf + m) % 8 * CHUNK + leaf // 8 * 112 + (6 - m) * 16
                gwp[pl.ds(pl.multiple_of(goal_at, 16), 16), :] = block[m * 16 : m * 16 + 16, :]

    def c_copy(n):
        cx = (mx + n) % 4
        return pltpu.make_async_remote_copy(
            src_ref=gwp.at[pl.ds(pl.multiple_of((2 * cx + 1 - mc) * CHUNK, 16), CHUNK)],
            dst_ref=cbuf.at[pl.ds(pl.multiple_of(cx * CHUNK, 16), CHUNK)],
            send_sem=c_ss.at[n], recv_sem=c_rs.at[n],
            device_id=(2 * mx + 1 - mc, ml), device_id_type=MESH,
        )

    for n in (2, 1, 3, 0):
        c_copy(n).start()

    forward_on(2)

    def chip_sum(n, half):
        cx = (mx + n) % 4
        a = gwp[pl.ds(pl.multiple_of((2 * cx + mc) * CHUNK + half * HALFC, 16), HALFC), :]
        b = cbuf[pl.ds(pl.multiple_of(cx * CHUNK + half * HALFC, 16), HALFC), :]
        return a + b

    up = (2 * ((mx + 1) % 4) + mc, ml)
    down = (2 * ((mx + 3) % 4) + mc, ml)

    def x_copy(n, src, dst, to):
        return pltpu.make_async_remote_copy(
            src_ref=src, dst_ref=dst, send_sem=x_ss.at[n], recv_sem=x_rs.at[n],
            device_id=to, device_id_type=MESH,
        )

    c_copy(2).wait()
    xsa[...] = chip_sum(2, 0).astype(BF)
    xsb[...] = chip_sum(2, 1).astype(BF)
    x0 = x_copy(0, xsa, xra, up)
    x0.start()
    x1 = x_copy(1, xsb, xrb, down)
    x1.start()
    forward_on(6)
    c_copy(1).wait()
    xsp[...] = chip_sum(1, 1).astype(BF)
    x2 = x_copy(2, xsp, xrp, up)
    x2.start()
    c_copy(3).wait()
    xsm[...] = chip_sum(3, 0).astype(BF)
    x3 = x_copy(3, xsm, xrm, down)
    x3.start()
    forward_on(1)
    c_copy(0).wait()
    x0.wait()
    xs2p[...] = (chip_sum(1, 0) + xra[...].astype(F32)).astype(BF)
    x4 = x_copy(4, xs2p, xr2p, up)
    x4.start()
    x1.wait()
    xs2m[...] = (chip_sum(3, 1) + xrb[...].astype(F32)).astype(BF)
    x5 = x_copy(5, xs2m, xr2m, down)
    x5.start()

    forward_on(7)
    forward_on(0)
    e2r[pl.ds(mz * 16, 16)] = e2m[pl.ds(mz * 16, 16)]

    @pl.loop(0, 2)
    def _(b):
        rows = pl.ds(pl.multiple_of(b * 256, 256), 256)
        for s in SHIFTS:
            ps = HOLD[s]
            first = FIRST[s] * 128
            part = lax.dot_general(
                gs[pl.ds(pl.multiple_of(s * 512 + b * 256, 256), 256), :],
                wr[first : first + 128 * len(ps), :],
                (((1,), (1,)), ((), ())),
                preferred_element_type=F32,
            )
            for n, p in enumerate(ps):
                piece = part[:, n * 128 : n * 128 + 128]
                if s == 0:
                    gx[rows, p * 128 : p * 128 + 128] = piece
                else:
                    gx[rows, p * 128 : p * 128 + 128] += piece

    @pl.loop(0, 8)
    def _(i):
        halves = []
        for h in range(2):
            rows = pl.ds(pl.multiple_of(i * 64, 64) + 32 * h, 32)
            halves.append(jnp.concatenate([gx[rows, p * 128 : p * 128 + 128] for p in range(8)], axis=0))
        block = jnp.concatenate(halves, axis=1).astype(BF)
        block = jnp.where(i < count, block, jnp.zeros((), BF))
        back_ = dot(permt[...], block).astype(BF)
        at = pl.multiple_of(i * 512, 512)
        gl[pl.ds(at, 256), :] = back_[:, 0:128]
        gl[pl.ds(at + 256, 256), :] = back_[:, 128:256]

    gl_out = pltpu.make_async_copy(gl, gl_h, out_sem.at[0])
    gl_out.start()

    @pl.loop(0, 2)
    def _(b):
        rows = pl.ds(pl.multiple_of(b * 256, 256), 256)
        e_int[rows, :] = dot(xc[rows, :], wr[0:1024, :])

    x3.wait()
    x4.wait()
    own[0:HALFC, :] = chip_sum(0, 0) + xrm[...].astype(F32) + xr2p[...].astype(F32)
    x2.wait()
    x5.wait()
    own[HALFC:CHUNK, :] = chip_sum(0, 1) + xrp[...].astype(F32) + xr2m[...].astype(F32)
    lsend[...] = own[...].astype(BF)

    def ly_copy(d):
        to = (my + d) % 4
        return remote(
            lsend.at[pl.ds(pl.multiple_of(to * 112, 16), 112)],
            lrecv.at[pl.ds(pl.multiple_of(my * 112, 16), 112)],
            ly_ss.at[d], ly_rs.at[d], at_y(d),
        )

    for d in (2, 1, 3):
        ly_copy(d).start()
    total = own[pl.ds(pl.multiple_of(my * 112, 16), 112), :]
    for d in (2, 1, 3):
        ly_copy(d).wait()
        came = (my + 4 - d) % 4
        total = total + lrecv[pl.ds(pl.multiple_of(came * 112, 16), 112), :].astype(F32)
    zsend[0:112, :] = total

    def block_for(z):
        return (z + 14 - ms) % 8

    def lz_copy(d):
        c = block_for((mz + d) % 8)
        return remote(
            zsend.at[pl.ds(pl.multiple_of(c * 16, 16), 16)],
            zrecv.at[pl.ds(pl.multiple_of(mz * 16, 16), 16)],
            lz_ss.at[d], lz_rs.at[d], at_z(d),
        )

    mine = block_for(mz)
    for d in FAR_FIRST[:7]:
        @pl.when(block_for((mz + d) % 8) != 7)
        def _():
            lz_copy(d).start()

    def f_copy(d):
        return remote(
            fs, frecv.at[pl.ds(pl.multiple_of((6 - mine) * 16, 16), 16)],
            f_ss.at[d], f_rs.at[d], ((ms + d) % 8, ml),
        )

    @pl.when(mine != 7)
    def _():
        for d in FAR_FIRST[:7]:
            lz_copy(d).wait_recv()
        total = zsend[pl.ds(pl.multiple_of(mine * 16, 16), 16), :]
        for d in range(1, 8):
            total = total + zrecv[pl.ds(pl.multiple_of((mz + d) % 8 * 16, 16), 16), :]
        fs[...] = total

        @pl.loop(1, 8)
        def _(d):
            f_copy(d).start()

        frecv[pl.ds(pl.multiple_of((6 - mine) * 16, 16), 16), :] = fs[...]

    for d in FAR_FIRST[:7]:
        @pl.when(block_for((mz + d) % 8) != 7)
        def _():
            lz_copy(d).wait_send()

    places.wait()
    for d in range(1, 8):
        eb_copy(d).wait()

    @pl.loop(0, 8)
    def _(i):
        for d in range(7):
            of[d * 16 : d * 16 + 16, :] = e2r[ids[2, i * 8 + d]]
        of[112:128, :] = jnp.zeros((16, 256), BF)
        rows = pl.ds(pl.multiple_of(i * 64, 64), 64)
        y = e_int[rows, :] + e5[pl.ds(pl.multiple_of(i * 128, 128), 64), :] + dot(facet[...], of[...])
        out[pl.ds(i * 16, 16)] = jnp.where(i < count, y, 0.0).astype(BF).reshape(16, 4, 256)

    out_out = pltpu.make_async_copy(out, out_h, out_sem.at[1])
    out_out.start()

    @pl.loop(1, 8)
    def _(d):
        @pl.when((mz + 14 - (ms + 8 - d) % 8) % 8 != 7)
        def _():
            came = (mz + 14 - (ms + 8 - d) % 8) % 8
            remote(
                fs, frecv.at[pl.ds(pl.multiple_of((6 - came) * 16, 16), 16)],
                f_ss.at[d], f_rs.at[d], ((ms + d) % 8, ml),
            ).wait_recv()

    @pl.when(mine != 7)
    def _():
        @pl.loop(1, 8)
        def _(d):
            f_copy(d).wait_send()

    gw[...] = frecv[0:108, :]
    gl_out.wait()
    out_out.wait()


def hand_over(*arrays):
    def copy(*refs):
        n = len(arrays)
        held, sem_in, sem_out = refs[2 * n : 3 * n], refs[3 * n], refs[3 * n + 1]
        into = [pltpu.make_async_copy(refs[k], held[k], sem_in.at[k]) for k in range(n)]
        onto = [pltpu.make_async_copy(held[k], refs[n + k], sem_out.at[k]) for k in range(n)]
        for one in into:
            one.start()
        for one, two in zip(into, onto):
            one.wait()
            two.start()
        for two in onto:
            two.wait()

    hbm = pl.BlockSpec(memory_space=pl.ANY)
    sems = pltpu.SemaphoreType.DMA
    return pl.pallas_call(
        copy,
        out_shape=tuple(jax.ShapeDtypeStruct(a.shape, a.dtype) for a in arrays),
        in_specs=[hbm] * len(arrays),
        out_specs=(hbm,) * len(arrays),
        scratch_shapes=[pltpu.VMEM(a.shape, a.dtype) for a in arrays] + [sems((len(arrays),)), sems((len(arrays),))],
    )(*arrays)


def per_device(leaves, counts, nbr_owner, nbr_slot, weight, cotangent):
    consts = [jnp.asarray(t, BF) for t in tables()]
    vmem = pl.BlockSpec(memory_space=pltpu.VMEM)
    hbm = pl.BlockSpec(memory_space=pl.ANY)
    sems = pltpu.SemaphoreType.DMA
    V = pltpu.VMEM
    out, gl, gw = pl.pallas_call(
        kernel,
        out_shape=(
            jax.ShapeDtypeStruct((128, 4, 256), BF),
            jax.ShapeDtypeStruct((4096, 128), BF),
            jax.ShapeDtypeStruct((108, 256), F32),
        ),
        in_specs=[pl.BlockSpec(memory_space=pltpu.SMEM)] * 3 + [hbm] * 11,
        out_specs=(hbm, hbm, vmem),
        scratch_shapes=[
            V((4096, 128), BF), V((128, 4, 256), BF), *[V(t.shape, BF) for t in consts], V((128, 4, 256), BF), V((4096, 128), BF),
            V((8, 128), jnp.int32), pltpu.SMEM((8, 128), jnp.int32), V((128, 128), jnp.int32), V((128, 128), jnp.int32),
            V((3456, 256), BF), V((512, 1024), BF), V((1024, 512), BF), V((1024, 2432), BF),
            V((512, 256), F32), V((1024, 256), F32), V((512, 256), BF), V((8, ROWS, 256), BF), V((64, 16, 256), BF),
            *[V((128, 16, 256), BF) for _ in range(5)],
            V((32, 1, 256), jnp.int32), pltpu.SMEM((32, 1, 256), jnp.int32),
            V((512, 256), F32), V((4096, 256), BF), V((512, 1024), F32), V((3472, 256), F32),
            V((8 * CHUNK, 256), F32), V((4 * CHUNK, 256), F32),
            *[V((HALFC, 256), BF) for _ in range(12)],
            V((CHUNK, 256), F32), V((CHUNK, 256), BF), V((CHUNK, 256), BF), V((128, 256), F32), V((128, 256), F32),
            V((16, 256), F32), V((128, 256), F32), V((128, 256), BF),
            sems((10,)), sems, sems, sems, sems((2,)), sems((16,)), sems((16,)), sems((8,)), sems((8,)), sems((4,)), sems((4,)),
            sems((32,)), sems((32,)), sems((32,)), sems((32,)), sems((8,)), sems((8,)),
            sems((4,)), sems((4,)), sems((6,)), sems((6,)), sems((4,)), sems((4,)), sems((8,)), sems((8,)),
            sems((8,)), sems((8,)),
        ],
        compiler_params=pltpu.CompilerParams(
            collective_id=0, has_side_effects=True, vmem_limit_bytes=56 * 1024 * 1024
        ),
        cost_estimate=pl.CostEstimate(flops=3 * 10**9, bytes_accessed=5 * 10**6, transcendentals=0),
    )(nbr_owner[0].T, nbr_slot[0].T, counts, leaves.reshape(4096, 128), cotangent.reshape(128, 4, 256), weight, *consts)
    out, gl, gw = hand_over(out, gl, gw)
    return (
        out.reshape(1, 8, 4, 4, 4, 256),
        gl.reshape(1, 8, 8, 8, 8, 128),
        gw,
    )


def solution(mesh):
    six = P("scene", "leaf", None, None, None, None)
    return jax.shard_map(
        per_device,
        mesh=mesh,
        in_specs=(six, P("scene", "leaf"), P("scene", "leaf", None), P("scene", "leaf", None), P(), six),
        out_specs=(six, six, P("leaf", None)),
        check_vma=False,
    )
```

```python
import functools

import jax
import jax.numpy as jnp
import numpy as np
from jax import lax
from jax.experimental import pallas as pl
from jax.experimental.pallas import tpu as pltpu
from jax.sharding import PartitionSpec as P

MESH = pl.DeviceIdType.MESH
BF = jnp.bfloat16
F32 = jnp.float32
CODES = (1, 2, 4, 3, 5, 6, 7)
SHIFTS = tuple(range(8))
CHUNK, HALFC = 448, 224
FAR_FIRST = (4, 3, 5, 2, 6, 1, 7, 0)
ROWS, PART = 304, 160
HOLD = {s: [p for p in range(8) if p & s == s] for s in SHIFTS}
FIRST = {}
_at = 0
for _s in SHIFTS:
    FIRST[_s] = _at
    _at += len(HOLD[_s])


def tap_of(parity, shift):
    t = 0
    for axis in range(3):
        if not parity >> axis & 1:
            digit = 1
        elif shift >> axis & 1:
            digit = 0
        else:
            digit = 2
        t = 3 * t + digit
    return t


ORDER = [tap_of(p, s) for s in SHIFTS for p in HOLD[s]]


def base_of(d):
    return 16 * d if d < 3 else 36 + 4 * d


def cells_of(d):
    code = CODES[d]
    ranges = [[None] if code >> axis & 1 else list(range(4)) for axis in range(3)]
    return [(i, j, k) for i in ranges[0] for j in ranges[1] for k in ranges[2]]


def tables():
    perm = np.zeros((256, 256), np.float32)
    for x in range(4):
        for y in range(8):
            for z in range(8):
                p = (x & 1) + 2 * (y & 1) + 4 * (z & 1)
                perm[p * 32 + (x >> 1) * 16 + (y >> 1) * 4 + (z >> 1), x * 64 + y * 8 + z] = 1
    facet = np.zeros((64, 128), np.float32)
    low_cells = [c for c in np.ndindex(4, 4, 4) if 0 in c]
    gather = np.zeros((ROWS, 512), np.float32)
    for leaf in range(8):
        for n, (x, y, z) in enumerate(low_cells):
            gather[leaf * 37 + n, leaf * 64 + 16 * x + 4 * y + z] = 1
    expand = np.zeros((64, 16, 384), np.float32)
    spread = np.zeros((128, 64), np.float32)
    place = {}
    for x in range(4):
        for y in range(4):
            for z in range(4):
                place[(x, y, z)] = 16 * x + 4 * y + z
    for d in range(7):
        for v, cell in enumerate(cells_of(d)):
            low = [0 if c is None else c for c in cell]
            facet[16 * low[0] + 4 * low[1] + low[2], d * 16 + v] = 1
            for leaf in range(8):
                expand[leaf * 8 + d, v, leaf * 37 + low_cells.index(tuple(low))] = 1
            spread[d * 16 + v, base_of(d) + v] = 1
            place[tuple(4 if c is None else c for c in cell)] = 64 + base_of(d) + v
    shift = np.zeros((7, 64, 128), np.float32)
    for s in range(1, 8):
        for x in range(4):
            for y in range(4):
                for z in range(4):
                    goal = (x + (s & 1), y + (s >> 1 & 1), z + (s >> 2 & 1))
                    shift[s - 1, 16 * x + 4 * y + z, place[goal]] = 1
    back = np.zeros((7, 512, 256), np.float32)
    for s in range(7):
        for leaf in range(4):
            back[s, leaf * 128 : leaf * 128 + 128, leaf * 64 : leaf * 64 + 64] = shift[s].T
    return (
        perm,
        perm.T.copy(),
        facet,
        spread,
        gather,
        expand,
        shift.reshape(448, 128),
        back.reshape(7 * 512, 256),
    )


def dot(a, b):
    return jnp.dot(a, b, preferred_element_type=F32)


def kernel(
    owners, slots, counts, leaves_h, cot_h, w_h, perm_h, permt_h, facet_h, spread_h, gather_h, expand_h, shift_h, back_h,
    out_h, gl_h, gw,
    leaves, cot, perm, permt, facet, spread, gather, expand, shift, back, out, gl,
    idv, ids, column, blocks, wr, xc, xt, xb, e_int, e5, gcot, ub, t128, e1s, e1r, e2s, e2m, e2r, codes, codes_sm,
    ghost, gs, gx, gwn, gwp, cbuf, xsa, xsb, xsp, xsm, xs2p, xs2m, xra, xrb, xrp, xrm, xr2p, xr2m,
    own, lsend, lrecv, zsend, zrecv, fs, frecv, of,
    in_sem, id_sem, w_sem, sm_sem, out_sem, ag_ss, ag_rs, iz_ss, iz_rs, iy_ss, iy_rs, e1_ss, e1_rs, ea_ss, ea_rs, eb_ss, eb_rs,
    c_ss, c_rs, x_ss, x_rs, ly_ss, ly_rs, lz_ss, lz_rs, f_ss, f_rs,
):
    ms = lax.axis_index("scene")
    ml = lax.axis_index("leaf")
    my, mz = ml // 8, ml % 8
    mx, mc = ms // 2, ms % 2
    count = counts[0, 0]

    def remote(src, dst, ss, rs, to):
        return pltpu.make_async_remote_copy(
            src_ref=src, dst_ref=dst, send_sem=ss, recv_sem=rs, device_id=to, device_id_type=MESH
        )

    def at_z(d):
        return (ms, my * 8 + (mz + d) % 8)

    def at_y(d):
        return (ms, (my + d) % 4 * 8 + mz)

    loads = [
        pltpu.make_async_copy(src, dst, in_sem.at[n])
        for n, (src, dst) in enumerate(
            (
                (cot_h, cot), (gather_h, gather), (leaves_h, leaves), (perm_h, perm), (expand_h, expand),
                (back_h, back), (spread_h, spread), (shift_h, shift), (permt_h, permt), (facet_h, facet),
            )
        )
    ]
    for load in loads[:4]:
        load.start()

    for n, t in enumerate(ORDER):
        pltpu.make_async_copy(
            w_h.at[pl.ds(t * 128, 128)], wr.at[pl.ds(n * 128, 128)], w_sem
        ).start()
    for load in loads[4:]:
        load.start()

    barrier = pltpu.get_barrier_semaphore()

    @pl.loop(1, 8)
    def _(d):
        pl.semaphore_signal(barrier, inc=1, device_id=at_z(d), device_id_type=MESH)
        pl.semaphore_signal(barrier, inc=1, device_id=((ms + d) % 8, ml), device_id_type=MESH)

    @pl.loop(1, 4)
    def _(d):
        pl.semaphore_signal(barrier, inc=1, device_id=at_y(d), device_id_type=MESH)

    loads[0].wait()

    @pl.loop(0, 8)
    def _(i):
        rows = pl.ds(pl.multiple_of(i * 64, 64), 64)
        gcot[rows, :] = jnp.where(i < count, cot[pl.ds(i * 16, 16)].reshape(64, 256), jnp.zeros((), BF))

    loads[1].wait()
    ub[mz] = dot(gather[...], gcot[...]).astype(BF)
    pl.semaphore_wait(barrier, 17)

    halves = (pl.ds(0, PART), pl.ds(PART, ROWS - PART))

    def ag_copy(way, half, hop):
        origin = (mz + 8 - (hop - 1)) % 8 if way == 0 else (mz + hop - 1) % 8
        block = ub.at[origin, halves[half]]
        n = (way * 2 + half) * 4 + hop - 1
        return remote(block, block, ag_ss.at[n], ag_rs.at[n], at_z(1 if way == 0 else 7))

    def iz_copy(d):
        return remote(codes.at[ml], codes.at[ml], iz_ss.at[d], iz_rs.at[d], at_z(d))

    def iy_copy(d):
        group = codes.at[pl.ds(my * 8, 8)]
        return remote(group, group, iy_ss.at[d], iy_rs.at[d], at_y(d))

    for way in range(2):
        for half in (way, 1 - way):
            ag_copy(way, half, 1).start()

    for n in range(64):
        i, d = n // 8, n % 8
        if d < 7:
            owner, block = owners[CODES[d] - 1, i], slots[CODES[d] - 1, i] * 8 + d
        else:
            owner, block = jnp.int32(99), jnp.int32(7)
        column[n : n + 1, :] = jnp.full((1, 128), owner, jnp.int32)
        blocks[n : n + 1, :] = jnp.full((1, 128), block, jnp.int32)
    column[64:128, :] = jnp.full((64, 128), 99, jnp.int32)
    blocks[64:128, :] = jnp.full((64, 128), 7, jnp.int32)
    down_n = lax.broadcasted_iota(jnp.int32, (128, 128), 0)
    along_n = lax.broadcasted_iota(jnp.int32, (128, 128), 1)
    owner_down = column[...]
    owner_along = owner_down.T
    same = jnp.where(owner_down == owner_along, 1, 0)
    rank_down = jnp.sum(jnp.where(along_n < down_n, same, 0), axis=1, keepdims=True)
    rank_along = jnp.sum(jnp.where(down_n < along_n, same, 0), axis=0, keepdims=True)
    hit = owner_down * 4 + rank_down == along_n
    own_row = owner_along[0:1, :]
    idv[0:1, :] = 7 + jnp.sum(jnp.where(hit, down_n - 7, 0), axis=0, keepdims=True)
    idv[1:2, :] = 7 + jnp.sum(jnp.where(hit, blocks[...] - 7, 0), axis=0, keepdims=True)
    idv[2:3, :] = ((own_row & 7) * 4 + (own_row >> 3)) * 4 + rank_along
    idv[3:8, :] = jnp.zeros((5, 128), jnp.int32)
    places = pltpu.make_async_copy(idv, ids, id_sem)
    places.start()

    codes[ml, :, 0:128] = idv[0:1, :]
    codes[ml, :, 128:256] = idv[1:2, :]

    @pl.loop(1, 8)
    def _(d):
        iz_copy(d).start()

    def hop_done(way, half, hop):
        ag_copy(way, half, hop).wait()
        if hop < (4 if half == way else 3):
            ag_copy(way, half, hop + 1).start()

    def hop_part(part, hop):
        hop_done(0, part, hop)
        hop_done(1, 1 - part, hop)

    hop_part(0, 1)
    loads[2].wait()
    loads[3].wait()

    @pl.loop(0, 8)
    def _(i):
        at = pl.multiple_of(i * 512, 512)
        block = jnp.concatenate([leaves[pl.ds(at, 256), :], leaves[pl.ds(at + 256, 256), :]], axis=1)
        block = jnp.where(i < count, block, jnp.zeros((), BF))
        sorted_ = dot(perm[...], block).astype(BF)
        for h in range(2):
            for p in range(8):
                xc[pl.ds(pl.multiple_of(i * 64, 64) + 32 * h, 32), p * 128 : p * 128 + 128] = sorted_[
                    p * 32 : p * 32 + 32, h * 128 : h * 128 + 128
                ]

    hop_part(1, 1)
    for p in range(8):
        xt[p * 128 : p * 128 + 128, :] = xc[:, p * 128 : p * 128 + 128].T

    @pl.loop(1, 8)
    def _(d):
        iz_copy(d).wait()

    for d in range(1, 4):
        iy_copy(d).start()
    group = pl.ds(my * 8, 8)
    to_sm = pltpu.make_async_copy(codes.at[group], codes_sm.at[group], sm_sem)
    to_sm.start()

    for load in loads[4:]:
        load.wait()

    def e1_copy(q, d):
        z = (mz + q) % 8
        to = (my + d) % 4
        return remote(
            e1s.at[pl.ds((z * 4 + to) * 4, 4)], e1r.at[pl.ds((z * 4 + my) * 4, 4)],
            e1_ss.at[q * 4 + d], e1_rs.at[q * 4 + d], at_y(d),
        )

    def serve(q):
        z = (mz + q) % 8
        picks = jnp.concatenate(
            [
                expand[codes_sm[my * 8 + z, 0, (y * 8 + mz) * 4 + k]]
                for y in range(4)
                for k in range(4)
            ],
            axis=0,
        )
        rows = dot(picks[:, 0:ROWS], ub[z]).astype(BF)
        e1s[pl.ds(z * 16, 16)] = rows.reshape(16, 16, 256)
        for d in range(1, 4):
            e1_copy(q, d).start()
        e1r[pl.ds((z * 4 + my) * 4, 4)] = e1s[pl.ds((z * 4 + my) * 4, 4)]

    def forward_shift(g):
        rows = pl.ds(g * 256, 256)
        for s in range(1, 8):
            ps = HOLD[s]
            for first in range(0, len(ps), 2):
                pair = ps[first : first + 2]
                block = jnp.concatenate([xc[rows, p * 128 : p * 128 + 128] for p in pair], axis=1)
                moved = dot(back[(s - 1) * 512 : s * 512, :], block).astype(BF)
                at = (FIRST[s] - 8 + first) * 128
                xb[pl.ds(g * 512, 512), at : at + 128 * len(pair)] = moved

    def forward_rows(b):
        e5[pl.ds(b * 256, 256), :] = dot(xb[pl.ds(b * 256, 256), :], wr[1024:3456, :])
        for i in (2 * b, 2 * b + 1):
            t64 = e5[pl.ds(i * 128 + 64, 64), :].astype(BF)
            t128[pl.ds(i * 8, 8)] = dot(spread[...], t64).astype(BF).reshape(8, 16, 256)

    def ea_copy(q, d):
        z = (mz + q) % 8
        to = (my + d) % 4
        return remote(
            e2s.at[pl.ds((to * 8 + z) * 4, 4)], e2m.at[pl.ds((z * 4 + my) * 4, 4)],
            ea_ss.at[q * 4 + d], ea_rs.at[q * 4 + d], at_y(d),
        )

    def eb_copy(d):
        z = (mz + d) % 8
        return remote(
            e2m.at[pl.ds(z * 16, 16)], e2r.at[pl.ds(mz * 16, 16)], eb_ss.at[d], eb_rs.at[d], at_z(d)
        )

    lane = lax.broadcasted_iota(jnp.int32, (1, 256), 1)
    goal = lax.broadcasted_iota(jnp.int32, (512, 256), 0)

    def gather_ghosts(q):
        z = (mz + q) % 8
        row = jnp.zeros((1, 256), jnp.int32)
        for y in range(4):
            for k in range(4):
                row = jnp.where(lane >> 4 == y * 4 + k, codes_sm[y * 8 + z, 0, 128 + ml * 4 + k], row)
        d = row & 7
        target = (row >> 3) * 64 + jnp.where(d < 3, 16 * d, 36 + 4 * d) + (lane & 15)
        pick = jnp.where(goal == target, 1.0, 0.0).astype(BF)
        for n in range(1, 4):
            e1_copy(q, n).wait()
        part = dot(pick, e1r[pl.ds(z * 16, 16)].reshape(256, 256))
        if q == 0:
            ghost[...] = part
        else:
            ghost[...] += part

    hop_part(0, 2)
    to_sm.wait()
    serve(0)
    pltpu.make_async_copy(w_h, wr, w_sem).wait()
    forward_shift(0)
    hop_part(1, 2)
    serve(7)
    serve(1)
    forward_shift(1)
    hop_part(0, 3)
    for d in range(1, 4):
        iy_copy(d).wait()
    all_sm = pltpu.make_async_copy(codes, codes_sm, sm_sem)
    all_sm.start()
    forward_rows(0)
    hop_part(1, 3)
    all_sm.wait()
    serve(6)
    serve(2)
    serve(5)
    serve(3)
    forward_rows(1)
    ag_copy(0, 0, 4).wait()
    ag_copy(1, 1, 4).wait()
    serve(4)
    forward_rows(2)
    forward_rows(3)

    @pl.loop(0, 32)
    def _(r):
        for k in range(4):
            e2s[r * 4 + k] = t128[codes_sm[r, 0, 128 + ml * 4 + k]]

    for q in FAR_FIRST:
        for d in range(1, 4):
            ea_copy(q, d).start()
    for z in range(8):
        e2m[pl.ds((z * 4 + my) * 4, 4)] = e2s[pl.ds((my * 8 + z) * 4, 4)]
    for q in (0, 7, 1, 6, 2, 5, 3, 4):
        gather_ghosts(q)

    def forward_on(q):
        for d in range(1, 4):
            ea_copy(q, d).wait()
        if q:
            eb_copy(q).start()

    forward_on(4)
    gs[0:512, :] = gcot[...]

    @pl.loop(0, 8)
    def _(i):
        rows = pl.ds(pl.multiple_of(i * 64, 64), 64)
        g5 = jnp.concatenate([gcot[rows, :], ghost[rows, :].astype(BF)], axis=0)
        moved = dot(shift[...], g5).astype(BF)
        for s in range(1, 8):
            gs[pl.ds(pl.multiple_of(s * 512 + i * 64, 64), 64), :] = moved[(s - 1) * 64 : s * 64, :]

    forward_on(3)
    gwn[3456:3472, :] = jnp.zeros((16, 256), F32)
    for s in SHIFTS:
        for p in HOLD[s]:
            t = tap_of(p, s)
            gwn[t * 128 : t * 128 + 128, :] = dot(
                xt[p * 128 : p * 128 + 128, :], gs[s * 512 : s * 512 + 512, :]
            )

    forward_on(5)

    @pl.loop(0, 16)
    def _(n):
        at = pl.multiple_of(n * 216, 8)
        even = gwn[pl.ds(at, 112), :]
        odd = gwn[pl.ds(pl.multiple_of(at + 104, 8), 120), :][4:116, :]
        for h, block in ((0, even), (1, odd)):
            leaf = 2 * n + h
            for m in range(7):
                goal_at = (leaf + m) % 8 * CHUNK + leaf // 8 * 112 + (6 - m) * 16
                gwp[pl.ds(pl.multiple_of(goal_at, 16), 16), :] = block[m * 16 : m * 16 + 16, :]

    def c_copy(n):
        cx = (mx + n) % 4
        return pltpu.make_async_remote_copy(
            src_ref=gwp.at[pl.ds(pl.multiple_of((2 * cx + 1 - mc) * CHUNK, 16), CHUNK)],
            dst_ref=cbuf.at[pl.ds(pl.multiple_of(cx * CHUNK, 16), CHUNK)],
            send_sem=c_ss.at[n], recv_sem=c_rs.at[n],
            device_id=(2 * mx + 1 - mc, ml), device_id_type=MESH,
        )

    for n in (2, 1, 3, 0):
        c_copy(n).start()

    forward_on(2)

    def chip_sum(n, half):
        cx = (mx + n) % 4
        a = gwp[pl.ds(pl.multiple_of((2 * cx + mc) * CHUNK + half * HALFC, 16), HALFC), :]
        b = cbuf[pl.ds(pl.multiple_of(cx * CHUNK + half * HALFC, 16), HALFC), :]
        return a + b

    up = (2 * ((mx + 1) % 4) + mc, ml)
    down = (2 * ((mx + 3) % 4) + mc, ml)

    def x_copy(n, src, dst, to):
        return pltpu.make_async_remote_copy(
            src_ref=src, dst_ref=dst, send_sem=x_ss.at[n], recv_sem=x_rs.at[n],
            device_id=to, device_id_type=MESH,
        )

    c_copy(2).wait()
    xsa[...] = chip_sum(2, 0).astype(BF)
    xsb[...] = chip_sum(2, 1).astype(BF)
    x0 = x_copy(0, xsa, xra, up)
    x0.start()
    x1 = x_copy(1, xsb, xrb, down)
    x1.start()
    forward_on(6)
    c_copy(1).wait()
    xsp[...] = chip_sum(1, 1).astype(BF)
    x2 = x_copy(2, xsp, xrp, up)
    x2.start()
    c_copy(3).wait()
    xsm[...] = chip_sum(3, 0).astype(BF)
    x3 = x_copy(3, xsm, xrm, down)
    x3.start()
    forward_on(1)
    c_copy(0).wait()
    x0.wait()
    xs2p[...] = (chip_sum(1, 0) + xra[...].astype(F32)).astype(BF)
    x4 = x_copy(4, xs2p, xr2p, up)
    x4.start()
    x1.wait()
    xs2m[...] = (chip_sum(3, 1) + xrb[...].astype(F32)).astype(BF)
    x5 = x_copy(5, xs2m, xr2m, down)
    x5.start()

    forward_on(7)
    forward_on(0)
    e2r[pl.ds(mz * 16, 16)] = e2m[pl.ds(mz * 16, 16)]

    @pl.loop(0, 2)
    def _(b):
        rows = pl.ds(pl.multiple_of(b * 256, 256), 256)
        for s in SHIFTS:
            ps = HOLD[s]
            first = FIRST[s] * 128
            part = lax.dot_general(
                gs[pl.ds(pl.multiple_of(s * 512 + b * 256, 256), 256), :],
                wr[first : first + 128 * len(ps), :],
                (((1,), (1,)), ((), ())),
                preferred_element_type=F32,
            )
            for n, p in enumerate(ps):
                piece = part[:, n * 128 : n * 128 + 128]
                if s == 0:
                    gx[rows, p * 128 : p * 128 + 128] = piece
                else:
                    gx[rows, p * 128 : p * 128 + 128] += piece

    @pl.loop(0, 8)
    def _(i):
        halves = []
        for h in range(2):
            rows = pl.ds(pl.multiple_of(i * 64, 64) + 32 * h, 32)
            halves.append(jnp.concatenate([gx[rows, p * 128 : p * 128 + 128] for p in range(8)], axis=0))
        block = jnp.concatenate(halves, axis=1).astype(BF)
        block = jnp.where(i < count, block, jnp.zeros((), BF))
        back_ = dot(permt[...], block).astype(BF)
        at = pl.multiple_of(i * 512, 512)
        gl[pl.ds(at, 256), :] = back_[:, 0:128]
        gl[pl.ds(at + 256, 256), :] = back_[:, 128:256]

    gl_out = pltpu.make_async_copy(gl, gl_h, out_sem.at[0])
    gl_out.start()

    @pl.loop(0, 2)
    def _(b):
        rows = pl.ds(pl.multiple_of(b * 256, 256), 256)
        e_int[rows, :] = dot(xc[rows, :], wr[0:1024, :])

    x3.wait()
    x4.wait()
    own[0:HALFC, :] = chip_sum(0, 0) + xrm[...].astype(F32) + xr2p[...].astype(F32)
    x2.wait()
    x5.wait()
    own[HALFC:CHUNK, :] = chip_sum(0, 1) + xrp[...].astype(F32) + xr2m[...].astype(F32)
    lsend[...] = own[...].astype(BF)

    def ly_copy(d):
        to = (my + d) % 4
        return remote(
            lsend.at[pl.ds(pl.multiple_of(to * 112, 16), 112)],
            lrecv.at[pl.ds(pl.multiple_of(my * 112, 16), 112)],
            ly_ss.at[d], ly_rs.at[d], at_y(d),
        )

    for d in (2, 1, 3):
        ly_copy(d).start()
    total = own[pl.ds(pl.multiple_of(my * 112, 16), 112), :]
    for d in (2, 1, 3):
        ly_copy(d).wait()
        came = (my + 4 - d) % 4
        total = total + lrecv[pl.ds(pl.multiple_of(came * 112, 16), 112), :].astype(F32)
    zsend[0:112, :] = total

    def block_for(z):
        return (z + 14 - ms) % 8

    def lz_copy(d):
        c = block_for((mz + d) % 8)
        return remote(
            zsend.at[pl.ds(pl.multiple_of(c * 16, 16), 16)],
            zrecv.at[pl.ds(pl.multiple_of(mz * 16, 16), 16)],
            lz_ss.at[d], lz_rs.at[d], at_z(d),
        )

    mine = block_for(mz)
    for d in FAR_FIRST[:7]:
        @pl.when(block_for((mz + d) % 8) != 7)
        def _():
            lz_copy(d).start()

    def f_copy(d):
        return remote(
            fs, frecv.at[pl.ds(pl.multiple_of((6 - mine) * 16, 16), 16)],
            f_ss.at[d], f_rs.at[d], ((ms + d) % 8, ml),
        )

    @pl.when(mine != 7)
    def _():
        for d in FAR_FIRST[:7]:
            lz_copy(d).wait_recv()
        total = zsend[pl.ds(pl.multiple_of(mine * 16, 16), 16), :]
        for d in range(1, 8):
            total = total + zrecv[pl.ds(pl.multiple_of((mz + d) % 8 * 16, 16), 16), :]
        fs[...] = total

        @pl.loop(1, 8)
        def _(d):
            f_copy(d).start()

        frecv[pl.ds(pl.multiple_of((6 - mine) * 16, 16), 16), :] = fs[...]

    for d in FAR_FIRST[:7]:
        @pl.when(block_for((mz + d) % 8) != 7)
        def _():
            lz_copy(d).wait_send()

    places.wait()
    for d in range(1, 8):
        eb_copy(d).wait()

    @pl.loop(0, 8)
    def _(i):
        for d in range(7):
            of[d * 16 : d * 16 + 16, :] = e2r[ids[2, i * 8 + d]]
        of[112:128, :] = jnp.zeros((16, 256), BF)
        rows = pl.ds(pl.multiple_of(i * 64, 64), 64)
        y = e_int[rows, :] + e5[pl.ds(pl.multiple_of(i * 128, 128), 64), :] + dot(facet[...], of[...])
        out[pl.ds(i * 16, 16)] = jnp.where(i < count, y, 0.0).astype(BF).reshape(16, 4, 256)

    out_out = pltpu.make_async_copy(out, out_h, out_sem.at[1])
    out_out.start()

    @pl.loop(1, 8)
    def _(d):
        @pl.when((mz + 14 - (ms + 8 - d) % 8) % 8 != 7)
        def _():
            came = (mz + 14 - (ms + 8 - d) % 8) % 8
            remote(
                fs, frecv.at[pl.ds(pl.multiple_of((6 - came) * 16, 16), 16)],
                f_ss.at[d], f_rs.at[d], ((ms + d) % 8, ml),
            ).wait_recv()

    @pl.when(mine != 7)
    def _():
        @pl.loop(1, 8)
        def _(d):
            f_copy(d).wait_send()

    gw[...] = frecv[0:108, :]
    gl_out.wait()
    out_out.wait()


def hand_over(*arrays):
    def copy(*refs):
        n = len(arrays)
        held, sem_in, sem_out = refs[2 * n : 3 * n], refs[3 * n], refs[3 * n + 1]
        into = [pltpu.make_async_copy(refs[k], held[k], sem_in.at[k]) for k in range(n)]
        onto = [pltpu.make_async_copy(held[k], refs[n + k], sem_out.at[k]) for k in range(n)]
        for one in into:
            one.start()
        for one, two in zip(into, onto):
            one.wait()
            two.start()
        for two in onto:
            two.wait()

    hbm = pl.BlockSpec(memory_space=pl.ANY)
    sems = pltpu.SemaphoreType.DMA
    return pl.pallas_call(
        copy,
        out_shape=tuple(jax.ShapeDtypeStruct(a.shape, a.dtype) for a in arrays),
        in_specs=[hbm] * len(arrays),
        out_specs=(hbm,) * len(arrays),
        scratch_shapes=[pltpu.VMEM(a.shape, a.dtype) for a in arrays] + [sems((len(arrays),)), sems((len(arrays),))],
    )(*arrays)


def per_device(leaves, counts, nbr_owner, nbr_slot, weight, cotangent):
    consts = [jnp.asarray(t, BF) for t in tables()]
    vmem = pl.BlockSpec(memory_space=pltpu.VMEM)
    hbm = pl.BlockSpec(memory_space=pl.ANY)
    sems = pltpu.SemaphoreType.DMA
    V = pltpu.VMEM
    out, gl, gw = pl.pallas_call(
        kernel,
        out_shape=(
            jax.ShapeDtypeStruct((128, 4, 256), BF),
            jax.ShapeDtypeStruct((4096, 128), BF),
            jax.ShapeDtypeStruct((108, 256), F32),
        ),
        in_specs=[pl.BlockSpec(memory_space=pltpu.SMEM)] * 3 + [hbm] * 11,
        out_specs=(hbm, hbm, vmem),
        scratch_shapes=[
            V((4096, 128), BF), V((128, 4, 256), BF), *[V(t.shape, BF) for t in consts], V((128, 4, 256), BF), V((4096, 128), BF),
            V((8, 128), jnp.int32), pltpu.SMEM((8, 128), jnp.int32), V((128, 128), jnp.int32), V((128, 128), jnp.int32),
            V((3456, 256), BF), V((512, 1024), BF), V((1024, 512), BF), V((1024, 2432), BF),
            V((512, 256), F32), V((1024, 256), F32), V((512, 256), BF), V((8, ROWS, 256), BF), V((64, 16, 256), BF),
            *[V((128, 16, 256), BF) for _ in range(5)],
            V((32, 1, 256), jnp.int32), pltpu.SMEM((32, 1, 256), jnp.int32),
            V((512, 256), F32), V((4096, 256), BF), V((512, 1024), F32), V((3472, 256), F32),
            V((8 * CHUNK, 256), F32), V((4 * CHUNK, 256), F32),
            *[V((HALFC, 256), BF) for _ in range(12)],
            V((CHUNK, 256), F32), V((CHUNK, 256), BF), V((CHUNK, 256), BF), V((128, 256), F32), V((128, 256), F32),
            V((16, 256), F32), V((128, 256), F32), V((128, 256), BF),
            sems((10,)), sems, sems, sems, sems((2,)), sems((16,)), sems((16,)), sems((8,)), sems((8,)), sems((4,)), sems((4,)),
            sems((32,)), sems((32,)), sems((32,)), sems((32,)), sems((8,)), sems((8,)),
            sems((4,)), sems((4,)), sems((6,)), sems((6,)), sems((4,)), sems((4,)), sems((8,)), sems((8,)),
            sems((8,)), sems((8,)),
        ],
        compiler_params=pltpu.CompilerParams(
            collective_id=0, has_side_effects=True, vmem_limit_bytes=56 * 1024 * 1024
        ),
        cost_estimate=pl.CostEstimate(flops=3 * 10**9, bytes_accessed=5 * 10**6, transcendentals=0),
    )(nbr_owner[0].T, nbr_slot[0].T, counts, leaves.reshape(4096, 128), cotangent.reshape(128, 4, 256), weight, *consts)
    out, gl, gw = hand_over(out, gl, gw)
    return (
        out.reshape(1, 8, 4, 4, 4, 256),
        gl.reshape(1, 8, 8, 8, 8, 128),
        gw,
    )


def solution(mesh):
    six = P("scene", "leaf", None, None, None, None)
    return jax.shard_map(
        per_device,
        mesh=mesh,
        in_specs=(six, P("scene", "leaf"), P("scene", "leaf", None), P("scene", "leaf", None), P(), six),
        out_specs=(six, six, P("leaf", None)),
        check_vma=False,
    )
```
